256 devices in a mesh: seq: 4 (over x), expert: 64 (over y, z, core).
Axes of the slice: x: 4, y: 4, z: 8, core: 2. Of those that a mesh axis runs over, the one named last changes fastest.
Arguments:
- tokens: bfloat16 [2048, 4096], P(('seq', 'expert')), may hold values from -6 to 6
- out_grad: bfloat16 [2048, 4096], P(('seq', 'expert')), may hold values from -6 to 6
- expert_ids: int32 [2048, 8], P(('seq', 'expert')), may hold values from 0 to 63, all different within a row; in each aligned block of 8 rows (0 to 7, 8 to 15, ...) at most 2 rows name the same one
- gate_values: bfloat16 [2048, 8], P(('seq', 'expert')), may hold values from 0.049804688 to 0.34960938
- gate_weight: bfloat16 [64, 768, 4096], P('expert', 'seq'), may hold values from -0.09375 to 0.09375
- up_weight: bfloat16 [64, 768, 4096], P('expert', 'seq'), may hold values from -0.09375 to 0.09375
- down_weight: bfloat16 [64, 768, 4096], P('expert', 'seq'), may hold values from -0.21875 to 0.21875
Outputs:
- token_grad: bfloat16 [2048, 4096], P(('seq', 'expert'))
- router_grad: float32 [2048, 8], P(('seq', 'expert'))
- grad_gate: bfloat16 [64, 768, 4096], P('expert', 'seq')
- grad_up: bfloat16 [64, 768, 4096], P('expert', 'seq')
- grad_down: bfloat16 [64, 768, 4096], P('expert', 'seq')
The draws below stay inside these ranges and needn't reach their ends.
Inputs may be any that keep to these rules, and one draw needn't show every extreme that they name: `expert_ids`: each row names 8 different experts; among the rows of one device no expert is named more than 2 times.
All inputs are finite; a program needn't handle non-finite values.
Results may differ from the reference program's by a relative error of at most 0.0075.
Values may be sent and summed in bfloat16 or wider, within the bound.
No kernel may reach another device: no remote copies, remote signals or barrier semaphores. Data moves between devices by JAX's collectives and lax.ppermute only.
A program may use at most 128 MiB of HBM per device.

```python
import math
import jax
import jax.numpy as jnp
import numpy as np
from jax import lax

D = 4096
FF = 768
TOPK = 8
TOK_DEV = 8
EXPERTS = 64
CAP = 2
TOKENS = 2048
N_SEQ = 4
N_EXPERT = 64


def levels(key, dims, cuts, least, largest):
    def one(dim, blocks):
        draws = jax.random.uniform(jax.random.fold_in(jax.random.fold_in(key, 6), dim), (blocks,), jnp.float32, least / len(cuts), largest / len(cuts))
        return jnp.repeat(jnp.exp(draws), dims[dim] // blocks).reshape((-1,) + (1,) * (len(dims) - dim - 1))

    loudness = one(*cuts[0])
    for cut in cuts[1:]:
        loudness = loudness * one(*cut)
    return loudness


def deal_out(stream_key, own, number, rows, amount, top, reach, lean):
    order = jax.random.permutation(stream_key, amount)
    heavy_load, usual = load_shares(amount, rows * top, reach, lean, True), load_shares(amount, rows * top, reach, lean, False)
    places = jnp.arange(amount)

    def named(lengths, rotation):
        used = int((lengths > 0).sum())
        fixed = max(1, used // 4)
        moved = fixed + (places - fixed + rotation * (used - fixed)) % max(1, amount - fixed)
        return jnp.zeros((amount,), jnp.int32).at[order[jnp.where(places < fixed, places, moved)]].set(jnp.asarray(lengths, jnp.int32))

    lengths = jnp.where(number % 4 == 0, named(heavy_load, number // 4), named(usual, number - number // 4 - 1))
    mixed = jax.random.permutation(jax.random.fold_in(own, 3), amount)
    giver, receiver = mixed[0:amount // 2 * 2:2], mixed[1:amount // 2 * 2:2]
    room = jnp.minimum(lengths[giver] - 1, reach - lengths[receiver]) // 2
    room = jnp.where((giver == order[0]) | (receiver == order[0]) | (lengths[receiver] == 0), 0, jnp.maximum(room, 0))
    moved = jax.random.randint(jax.random.fold_in(own, 4), (amount // 2,), 0, 1 << 20) % (room + 1)
    lengths = lengths.at[giver].add(-moved).at[receiver].add(moved)
    items = jnp.searchsorted(jnp.cumsum(lengths), jnp.arange(rows * top), side="right").astype(jnp.int32)
    grid = items.reshape(top, rows).T
    grid = grid[jax.random.permutation(jax.random.fold_in(own, 1), rows)]
    rotation = jax.random.randint(jax.random.fold_in(own, 2), (rows, 1), 0, top)
    return jnp.take_along_axis(grid, (jnp.arange(top)[None, :] + rotation) % top, axis=1)


def load_shares(amount, total, most, slope, full):
    loads = [(1 << 20) // math.isqrt(standing ** slope) + 1 for standing in range(1, amount + 1)]
    largest = most if full else min(most, max(-(-total // amount), total * loads[0] // sum(loads)))
    least = 1 if total - largest >= amount - 1 else 0
    counts, rest = [largest] + [least] * (amount - 1), total - largest - least * (amount - 1)
    while rest > 0:
        free = [i for i in range(1, amount) if counts[i] < largest] or [i for i in range(1, amount) if counts[i] < most]
        mass, budget = sum([loads[i] for i in free]), rest
        for i in free:
            more = min(most - counts[i], max(1, budget * loads[i] // mass), rest)
            counts[i] = counts[i] + more
            rest = rest - more
    return np.array(counts)


def centred(own_key, dims, spread, bound, pieces=(), kind=jnp.bfloat16):
    drawn = spread * jax.random.normal(own_key, dims, jnp.float32)
    if pieces:
        drawn = drawn * levels(own_key, dims, pieces, -0.22, 0.18)
    return jnp.clip(drawn, -bound, bound).astype(kind)


def setup_inputs(seed: int = 0) -> dict:
    arg_keys = jax.random.split(jax.random.key(seed), 8)
    tokens = centred(arg_keys[0], (TOKENS, D), 1.0, 6.0, ((0, 256),))
    out_grad = centred(arg_keys[1], (TOKENS, D), 1.0, 6.0, ((0, 256),))
    expert_ids_keys = jax.random.split(jax.random.fold_in(arg_keys[2], 1), TOKENS // TOK_DEV)
    expert_ids_turns = jax.random.permutation(jax.random.fold_in(arg_keys[2], 3), TOKENS // TOK_DEV)
    expert_ids = jax.vmap(lambda own, number: deal_out(jax.random.fold_in(arg_keys[2], 2), own, number, TOK_DEV, EXPERTS, TOPK, CAP, 2))(expert_ids_keys, expert_ids_turns).reshape((TOKENS, TOPK))
    gate_values = jnp.clip(0.049804688 + 0.2998047 * jax.random.uniform(arg_keys[3], (TOKENS, TOPK), jnp.float32) ** levels(arg_keys[3], (TOKENS, TOPK), ((0, 256),), -0.2, 0.2), 0.049804688, 0.34960938).astype(jnp.bfloat16)
    gate_weight = centred(arg_keys[4], (EXPERTS, FF, D), D ** -0.5, 0.09375, ((0, 64), (1, 4)))
    up_weight = centred(arg_keys[5], (EXPERTS, FF, D), D ** -0.5, 0.09375, ((0, 64), (1, 4)))
    down_weight = centred(arg_keys[6], (EXPERTS, FF, D), FF ** -0.5, 0.21875, ((0, 64), (1, 4)))
    return {"tokens": tokens, "out_grad": out_grad, "expert_ids": expert_ids, "gate_values": gate_values, "gate_weight": gate_weight, "up_weight": up_weight, "down_weight": down_weight}


def reference(tokens, out_grad, expert_ids, gate_values, gate_weight, up_weight, down_weight):
    assign_total = TOKENS * TOPK
    buffer = N_SEQ * N_EXPERT * CAP
    flat_ids = expert_ids.reshape(assign_total)
    token_of = jnp.arange(assign_total, dtype=jnp.int32) // TOPK
    flat_gates = gate_values.reshape(assign_total).astype(jnp.float32)
    contract_rows = (((0,), (0,)), ((), ()))
    contract_cols = (((1,), (1,)), ((), ()))

    def per_expert(carry, expert):
        grad_tokens, grad_router = carry
        chosen = (flat_ids == expert).astype(jnp.int32)
        position = (jnp.cumsum(chosen) - 1).astype(jnp.int32)
        target = jnp.where(chosen > 0, position, buffer).astype(jnp.int32)
        source_index = jnp.zeros((buffer,), jnp.int32).at[target].set(jnp.arange(assign_total, dtype=jnp.int32), mode="drop")
        filled_count = jnp.zeros((buffer,), jnp.int32).at[target].set(1, mode="drop")
        valid_mask = filled_count > 0
        token_rows = token_of[source_index]
        keep_mask = valid_mask[:, None]
        inputs = jnp.where(keep_mask, tokens[token_rows], jnp.zeros((), jnp.bfloat16))
        upstream = jnp.where(keep_mask, out_grad[token_rows], jnp.zeros((), jnp.bfloat16))
        weights = jnp.where(valid_mask, flat_gates[source_index], jnp.zeros((), jnp.float32))
        gate_matrix = gate_weight[expert]
        up_matrix = up_weight[expert]
        down_matrix = down_weight[expert]
        pre_gate = lax.dot_general(inputs, gate_matrix, contract_cols, preferred_element_type=jnp.float32)
        pre_up = lax.dot_general(inputs, up_matrix, contract_cols, preferred_element_type=jnp.float32)
        sigmoid_gate = jax.nn.sigmoid(pre_gate)
        activated = pre_gate * sigmoid_gate
        hidden = (activated * pre_up).astype(jnp.bfloat16)
        plain = lax.dot_general(upstream, down_matrix, contract_cols, preferred_element_type=jnp.float32)
        partial_router = jnp.sum(hidden.astype(jnp.float32) * plain, axis=1)
        scaled = (weights[:, None] * upstream.astype(jnp.float32)).astype(jnp.bfloat16)
        down_delta = lax.dot_general(hidden, scaled, contract_rows, preferred_element_type=jnp.float32).astype(jnp.bfloat16)
        grad_hidden = weights[:, None] * plain
        slope_term = sigmoid_gate * (1.0 + pre_gate * (1.0 - sigmoid_gate))
        delta_gate = (grad_hidden * pre_up * slope_term).astype(jnp.bfloat16)
        delta_up = (grad_hidden * activated).astype(jnp.bfloat16)
        gate_delta = lax.dot_general(delta_gate, inputs, contract_rows, preferred_element_type=jnp.float32).astype(jnp.bfloat16)
        up_delta = lax.dot_general(delta_up, inputs, contract_rows, preferred_element_type=jnp.float32).astype(jnp.bfloat16)
        back_rows = jnp.dot(delta_gate, gate_matrix, preferred_element_type=jnp.float32)
        back_rows = back_rows + jnp.dot(delta_up, up_matrix, preferred_element_type=jnp.float32)
        grad_tokens = grad_tokens.at[token_rows].add(jnp.where(keep_mask, back_rows, jnp.zeros((), jnp.float32)))
        grad_router = grad_router.at[source_index].add(jnp.where(valid_mask, partial_router, jnp.zeros((), jnp.float32)))
        return (grad_tokens, grad_router), (gate_delta, up_delta, down_delta)

    start = (jnp.zeros((TOKENS, D), jnp.float32), jnp.zeros((assign_total,), jnp.float32))
    (grad_tokens, grad_router), (grad_gate, grad_up, grad_down) = lax.scan(per_expert, start, jnp.arange(EXPERTS, dtype=jnp.int32))
    return (grad_tokens.astype(jnp.bfloat16), grad_router.reshape(TOKENS, TOPK), grad_gate, grad_up, grad_down)
```

```python
import jax
import jax.numpy as jnp
from jax import lax
from jax.sharding import PartitionSpec as P

NY, NZ, NC = 4, 8, 2
Z_ORDER = (0, -1, 1, -2, 2, -3, 3, 4)
Y_ORDER = (0, 1, -1, 2)
CAP = 2
PAD = 128
BF = jnp.bfloat16
F32 = jnp.float32


def move(v, dy=0, dz=0, dc=0):
    pairs = []
    for y in range(NY):
        for z in range(NZ):
            for c in range(NC):
                to = (((y + dy) % NY) * NZ + (z + dz) % NZ) * NC + (c + dc) % NC
                pairs.append(((y * NZ + z) * NC + c, to))
    return lax.ppermute(v, "expert", pairs)


def move_x(v, d):
    n = lax.axis_size("seq")
    return lax.ppermute(v, "seq", [(i, (i + d) % n) for i in range(n)])


def split_two(v):
    hi = lax.reduce_precision(v, 8, 7)
    return hi.astype(BF), (v - hi).astype(BF)


def body(tokens, out_grad, expert_ids, gate_values, gate_weight, up_weight, down_weight):
    rows, width = tokens.shape
    top = expert_ids.shape[1]
    share = gate_weight.shape[1]
    me = lax.axis_index("expert")
    my_y, my_zc = me // (NZ * NC), me % (NZ * NC)

    extra = jnp.concatenate(
        [expert_ids.astype(BF), gate_values, jnp.zeros((rows, PAD - 2 * top), BF)], axis=1
    )
    pay = jnp.concatenate([tokens, out_grad, extra], axis=1)

    have = {0: pay}
    ahead = back = pay
    for step in range(1, NZ // 2):
        ahead = move(ahead, dz=1)
        back = move(back, dz=-1)
        have[-step], have[step] = ahead, back
    have[NZ // 2] = jnp.concatenate(
        [move(ahead[:, :width], dz=1), move(back[:, width:], dz=-1)], axis=1
    )
    mine = jnp.concatenate([have[d] for d in Z_ORDER], axis=0)
    pool = jnp.concatenate([mine, move(mine, dc=1)], axis=0)
    count = pool.shape[0]

    ids = pool[:, 2 * width : 2 * width + top].astype(jnp.int32)
    r_at = lax.broadcasted_iota(jnp.int32, (count, count), 0)
    c_at = lax.broadcasted_iota(jnp.int32, (count, count), 1)
    before = ((r_at // rows == c_at // rows) & (c_at < r_at)).astype(BF)
    targets = [((my_y + d) % NY) * (NZ * NC) + my_zc for d in Y_ORDER]
    hits = [ids == t for t in targets]
    chosen = jnp.stack([jnp.any(h, axis=1) for h in hits], axis=1)
    place = jnp.dot(before, chosen.astype(BF), preferred_element_type=F32).astype(jnp.int32)
    place = place + (lax.broadcasted_iota(jnp.int32, place.shape, 0) // rows) * CAP
    slots = count // rows * CAP
    slot_of = jnp.where(chosen, place, -1)
    s_at = lax.broadcasted_iota(jnp.int32, (count, slots), 1)
    pick = jnp.concatenate(
        [(slot_of[:, i : i + 1] == s_at).astype(BF) for i in range(NY)], axis=1
    )
    picked = lax.dot_general(
        pick, pool, (((0,), (0,)), ((), ())), preferred_element_type=F32
    ).astype(BF)

    joined = jnp.concatenate([gate_weight[0], up_weight[0]], axis=0)
    down = down_weight[0]
    contract_cols = (((1,), (1,)), ((), ()))
    contract_rows = (((0,), (0,)), ((), ()))
    half = slots // 2
    parts, hiddens, deltas, returned = [], [], [], []
    for i, d in enumerate(Y_ORDER):
        own = picked[i * slots : (i + 1) * slots]
        if d:
            own = move(own, dy=d)
        left = move_x(own, 1)
        right = move_x(own, -1)
        far = [move_x(left[:half], 1), move_x(right[half:], -1)]
        part = jnp.concatenate([own, left, right] + far, axis=0)
        x, dy = part[:, :width], part[:, width : 2 * width]
        route = part[:, 2 * width :].astype(F32)
        gate = jnp.sum(
            jnp.where(route[:, :top] == me.astype(F32), route[:, top : 2 * top], 0.0),
            axis=1,
            keepdims=True,
        )
        pre = lax.dot_general(x, joined, contract_cols, preferred_element_type=F32)
        plain = lax.dot_general(dy, down, contract_cols, preferred_element_type=F32)
        pre_gate, pre_up = pre[:, :share], pre[:, share:]
        sig = jax.nn.sigmoid(pre_gate)
        act = pre_gate * sig
        hidden = act * pre_up
        router = jnp.sum(hidden.astype(BF).astype(F32) * plain, axis=1, keepdims=True)
        grad_hidden = gate * plain
        slope = sig * (1.0 + pre_gate * (1.0 - sig))
        delta = jnp.concatenate(
            [(grad_hidden * pre_up * slope).astype(BF), (grad_hidden * act).astype(BF)], axis=1
        )
        parts.append(part)
        hiddens.append((gate * hidden).astype(BF))
        deltas.append(delta)
        rows_back = jnp.dot(delta, joined, preferred_element_type=F32)

        def pack(vals, r):
            hi, lo = split_two(r)
            tail = jnp.concatenate([hi, lo, jnp.zeros((vals.shape[0], PAD - 2), BF)], axis=1)
            return jnp.concatenate([vals.astype(BF), tail], axis=1)

        def unpack(p):
            f = p[:, width : width + 2].astype(F32)
            return p[:, :width].astype(F32), f[:, :1] + f[:, 1:2]

        def block(a, b):
            return rows_back[a:b], router[a:b]

        far_at = 3 * slots
        via_left = move_x(pack(*block(far_at, far_at + half)), 1)
        via_right = move_x(pack(*block(far_at + half, far_at + slots)), -1)
        vl, rl = unpack(via_left)
        vr, rr = unpack(via_right)
        to_right = jnp.concatenate(
            [
                pack(rows_back[2 * slots : 2 * slots + half] + vl, router[2 * slots : 2 * slots + half] + rl),
                pack(*block(2 * slots + half, 3 * slots)),
            ],
            axis=0,
        )
        to_left = jnp.concatenate(
            [
                pack(*block(slots, slots + half)),
                pack(rows_back[slots + half : 2 * slots] + vr, router[slots + half : 2 * slots] + rr),
            ],
            axis=0,
        )
        va, ra = unpack(move_x(to_right, 1))
        vb, rb = unpack(move_x(to_left, -1))
        total = pack(rows_back[:slots] + va + vb, router[:slots] + ra + rb)
        returned.append(move(total, dy=-d) if d else total)

    home = jnp.concatenate(returned, axis=0)
    grads = jnp.dot(pick, home[:, :width], preferred_element_type=F32)
    routed = jnp.zeros((count, top), F32)
    for i in range(NY):
        val = jnp.dot(
            pick[:, i * slots : (i + 1) * slots], returned[i][:, width:], preferred_element_type=F32
        )
        routed = routed + jnp.where(hits[i], val[:, :1] + val[:, 1:2], 0.0)

    def pack_home(vals, r):
        hi, lo = split_two(r)
        return jnp.concatenate(
            [vals.astype(BF), hi, lo, jnp.zeros((vals.shape[0], PAD - 2 * top), BF)], axis=1
        )

    def unpack_home(p):
        f = p[:, width : width + 2 * top].astype(F32)
        return p[:, :width].astype(F32), f[:, :top] + f[:, top:]

    ours = count // NC
    va, ra = unpack_home(move(pack_home(grads[ours:], routed[ours:]), dc=1))
    cored = pack_home(grads[:ours] + va, routed[:ours] + ra)
    token_grad, router_grad = unpack_home(cored[:rows])
    for b, d in enumerate(Z_ORDER):
        if d:
            v, r = unpack_home(move(cored[b * rows : (b + 1) * rows], dz=d))
            token_grad = token_grad + v
            router_grad = router_grad + r

    every = jnp.concatenate(parts, axis=0)
    delta = jnp.concatenate(deltas, axis=0)
    weight_delta = lax.dot_general(
        delta, every[:, :width], contract_rows, preferred_element_type=F32
    ).astype(BF)
    down_delta = lax.dot_general(
        jnp.concatenate(hiddens, axis=0),
        every[:, width : 2 * width],
        contract_rows,
        preferred_element_type=F32,
    ).astype(BF)
    return (
        token_grad.astype(BF),
        router_grad,
        weight_delta[None, :share],
        weight_delta[None, share:],
        down_delta[None],
    )


def solution(mesh):
    both = P(("seq", "expert"), None)
    weight = P("expert", "seq", None)
    return jax.shard_map(
        body,
        mesh=mesh,
        in_specs=(both, both, both, both, weight, weight, weight),
        out_specs=(both, both, weight, weight, weight),
        check_vma=False,
    )
```

```python
import jax
import jax.numpy as jnp
from jax import lax
from jax.experimental import pallas as pl
from jax.experimental.pallas import tpu as pltpu
from jax.sharding import PartitionSpec as P

NY, NZ, NC = 4, 8, 2
Z_ORDER = (0, -1, 1, -2, 2, -3, 3, 4)
Y_ORDER = (0, 1, -1, 2)
CAP = 2
PAD = 128
BF = jnp.bfloat16
F32 = jnp.float32
COLS = (((1,), (1,)), ((), ()))
ROWS = (((0,), (0,)), ((), ()))
VMEM = pl.BlockSpec(memory_space=pltpu.VMEM)
SMEM = pl.BlockSpec(memory_space=pltpu.SMEM)


def dot(a, b, dims=(((1,), (0,)), ((), ()))):
    return lax.dot_general(a, b, dims, preferred_element_type=F32)


def tile(n, most):
    return max(b for b in range(PAD, most + 1, PAD) if n % b == 0)


def call(kernel, outs, args, flops, moved, scratch=(), **more):
    specs = dict(
        in_specs=[SMEM if a.dtype == jnp.int32 else VMEM for a in args],
        out_specs=[VMEM] * len(outs),
        scratch_shapes=list(scratch),
    )
    specs.update(more)
    return pl.pallas_call(
        kernel,
        out_shape=[jax.ShapeDtypeStruct(s, d) for s, d in outs],
        compiler_params=pltpu.CompilerParams(vmem_limit_bytes=44 * 2**20),
        cost_estimate=pl.CostEstimate(flops=flops, bytes_accessed=moved, transcendentals=0),
        **specs,
    )(*args)


def move(v, dy=0, dz=0, dc=0):
    pairs = []
    for y in range(NY):
        for z in range(NZ):
            for c in range(NC):
                to = (((y + dy) % NY) * NZ + (z + dz) % NZ) * NC + (c + dc) % NC
                pairs.append(((y * NZ + z) * NC + c, to))
    return lax.ppermute(v, "expert", pairs)


def move_x(v, d):
    n = lax.axis_size("seq")
    return lax.ppermute(v, "seq", [(i, (i + d) % n) for i in range(n)])


def lanes(shape):
    return lax.broadcasted_iota(jnp.int32, shape, 1)


def one_hot(slot, slots):
    at = lanes(slot.shape)
    pick = jnp.zeros(slot.shape, F32)
    for d in range(NY):
        of = jnp.sum(jnp.where(at == d, slot, 0.0), axis=1, keepdims=True)
        pick = jnp.where(of == (at - d * slots).astype(F32), 1.0, pick)
    return pick.astype(BF)


def choose(rows, top, width, block, targets, mine, other, s0, s1, s2, s3, slot_out, ids_out):
    count = 2 * mine.shape[0]
    slots = s0.shape[0]
    tail = jnp.concatenate([mine[:, 2 * width :], other[:, 2 * width :]], axis=0).astype(F32)
    at = lanes(tail.shape)
    row = lax.broadcasted_iota(jnp.int32, tail.shape, 0)
    ids = jnp.where(at < top, tail, -1.0)
    chosen = jnp.zeros(tail.shape, F32)
    for d in range(NY):
        hit = jnp.where(ids == targets[d].astype(F32), 1.0, 0.0)
        chosen = jnp.where(at == d, jnp.max(hit, axis=1, keepdims=True), chosen)
    before = jnp.where((row // rows == at // rows) & (at < row), 1.0, 0.0).astype(BF)
    place = dot(before, chosen.astype(BF))
    slot = jnp.where(chosen > 0.0, place + (row // rows * CAP).astype(F32), -4.0 * PAD)
    slot_out[...] = slot
    ids_out[...] = ids
    pick = one_hot(slot, slots)
    top_half, low_half = pick[: count // 2], pick[count // 2 :]
    outs = (s0, s1, s2, s3)
    for j in range(0, mine.shape[1], block):
        part = dot(top_half, mine[:, j : j + block], ROWS)
        part = (part + dot(low_half, other[:, j : j + block], ROWS)).astype(BF)
        for d in range(NY):
            outs[d][:, j : j + block] = part[d * slots : (d + 1) * slots]


def expert(top, block, me, own, left, right, fa, fb, wg, wu, wd, part, r_own, r_left, r_right, r_far, hg, dg, du):
    n = own.shape[0]
    width = wg.shape[1]
    part[:n] = own[...]
    part[n : 2 * n] = left[...]
    part[2 * n : 3 * n] = right[...]
    part[3 * n : 3 * n + n // 2] = fa[...]
    part[3 * n + n // 2 :] = fb[...]
    tail = part[:, 2 * width :].astype(F32)
    gates = pltpu.roll(tail, PAD - top, 1)
    mask = (tail == me[0].astype(F32)) & (lanes(tail.shape) < top)
    gate = jnp.sum(jnp.where(mask, gates, 0.0), axis=1, keepdims=True)
    x = part[:, :width]
    pre_gate = dot(x, wg[...], COLS)
    pre_up = dot(x, wu[...], COLS)
    plain = dot(part[:, width : 2 * width], wd[...], COLS)
    sig = jax.nn.sigmoid(pre_gate)
    act = pre_gate * sig
    hidden = act * pre_up
    router = jnp.sum(hidden.astype(BF).astype(F32) * plain, axis=1, keepdims=True)
    grad_hidden = gate * plain
    d_gate = (grad_hidden * pre_up * (sig * (1.0 + pre_gate * (1.0 - sig)))).astype(BF)
    d_up = (grad_hidden * act).astype(BF)
    hg[...] = (gate * hidden).astype(BF)
    dg[...] = d_gate
    du[...] = d_up
    outs = (r_own, r_left, r_right, r_far)
    for j in range(0, width, block):
        back = dot(d_gate, wg[:, j : j + block]) + dot(d_up, wu[:, j : j + block])
        for i, out in enumerate(outs):
            out[:, j : j + block] = back[i * n : (i + 1) * n].astype(out.dtype)
    wide = jnp.broadcast_to(router, (4 * n, PAD))
    for i, out in enumerate(outs):
        out[:, width:] = wide[i * n : (i + 1) * n].astype(out.dtype)


def combine(width, block, targets, slot, ids, h0, h1, h2, h3, keep, send, home):
    slots = h0.shape[0]
    half = keep.shape[0]
    for d, h in enumerate((h0, h1, h2, h3)):
        home[d * slots : (d + 1) * slots] = h[...]
    pick = one_hot(slot[...], slots)
    for j in range(0, width, block):
        part = dot(pick, home[:, j : j + block])
        keep[:, j : j + block] = part[:half]
        send[:, j : j + block] = part[half:].astype(BF)
    at = lanes(pick.shape)
    routed = jnp.zeros(slot.shape, F32)
    for d in range(NY):
        val = dot(jnp.where(at // slots == d, pick, jnp.zeros_like(pick)), home[:, width:])
        routed = routed + jnp.where(ids[...] == targets[d].astype(F32), val, 0.0)
    keep[:, width:] = routed[:half]
    send[:, width:] = routed[half:].astype(BF)


def outer(xa, xb, xc, ya, yb, yc, ga, gb, gc, ua, ub, uc, ha, hb, hc, o_gate, o_up, o_down):
    xs = (xa[...], xb[...], xc[...])
    ys = (ya[...], yb[...], yc[...])
    o_gate[...] = sum(dot(d[...], x, ROWS) for d, x in zip((ga, gb, gc), xs)).astype(BF)
    o_up[...] = sum(dot(d[...], x, ROWS) for d, x in zip((ua, ub, uc), xs)).astype(BF)
    o_down[...] = sum(dot(h[...], y, ROWS) for h, y in zip((ha, hb, hc), ys)).astype(BF)


def body(tokens, out_grad, expert_ids, gate_values, gate_weight, up_weight, down_weight):
    rows, width = tokens.shape
    top = expert_ids.shape[1]
    share = gate_weight.shape[1]
    full, back_w = 2 * width + PAD, width + PAD
    me = lax.axis_index("expert").astype(jnp.int32)
    my_y, my_zc = me // (NZ * NC), me % (NZ * NC)
    targets = jnp.stack([((my_y + d) % NY) * (NZ * NC) + my_zc for d in Y_ORDER])
    me = me[None]
    wg, wu, wd = gate_weight[0], up_weight[0], down_weight[0]

    extra = jnp.concatenate(
        [expert_ids.astype(BF), gate_values, jnp.zeros((rows, PAD - 2 * top), BF)], axis=1
    )
    pay = jnp.concatenate([tokens, out_grad, extra], axis=1)

    have = {0: pay}
    ahead = behind = pay
    for step in range(1, NZ // 2):
        ahead = move(ahead, dz=1)
        behind = move(behind, dz=-1)
        have[-step], have[step] = ahead, behind
    have[NZ // 2] = jnp.concatenate(
        [move(ahead[:, :width], dz=1), move(behind[:, width:], dz=-1)], axis=1
    )
    mine = jnp.concatenate([have[d] for d in Z_ORDER], axis=0)
    other = move(mine, dc=1)
    count = 2 * rows * NZ
    slots = count // rows * CAP

    def choose_k(*refs):
        choose(rows, top, width, tile(full, 1664), *refs)

    s0, s1, s2, s3, slot, ids = call(
        choose_k,
        [((slots, full), BF)] * NY + [((count, PAD), F32)] * 2,
        (targets, mine, other),
        2 * count * NY * slots * full,
        2 * count * full * 2,
    )
    chunks = [
        s0,
        jnp.concatenate([move(s1, dy=1), move(s2, dy=-1)], axis=0),
        move(s3, dy=2),
    ]

    def expert_k(*refs):
        expert(top, tile(width, 1024), *refs)

    saved, returned = [], []
    for own in chunks:
        n = own.shape[0]
        left, right = move_x(own, 1), move_x(own, -1)
        fa, fb = move_x(left[: n // 2], 1), move_x(right[n // 2 :], -1)
        part, r_own, r_left, r_right, r_far, hg, dg, du = call(
            expert_k,
            [((4 * n, full), BF), ((n, back_w), F32)]
            + [((n, back_w), BF)] * 3
            + [((4 * n, share), BF)] * 3,
            (me, own, left, right, fa, fb, wg, wu, wd),
            2 * 4 * n * width * share * 5,
            2 * (8 * n * full + 4 * n * back_w + 3 * share * width),
        )
        saved.append((part, hg, dg, du))
        total = (
            r_own
            + move_x(r_left, -1).astype(F32)
            + move_x(r_right, 1).astype(F32)
            + move_x(r_far, 2).astype(F32)
        )
        returned.append(total.astype(BF))

    def combine_k(*refs):
        combine(width, tile(width, 1024), *refs)

    keep, send = call(
        combine_k,
        [((count // NC, back_w), F32), ((count // NC, back_w), BF)],
        (
            targets,
            slot,
            ids,
            returned[0],
            move(returned[1][:slots], dy=-1),
            move(returned[1][slots:], dy=1),
            move(returned[2], dy=2),
        ),
        2 * count * count * back_w,
        10 * count * back_w // 2,
        scratch=[pltpu.VMEM((count, back_w), BF)],
    )
    cored = keep + move(send, dc=1).astype(F32)
    sent = cored.astype(BF)
    summed = cored[:rows]
    for b, d in enumerate(Z_ORDER):
        if d:
            summed = summed + move(sent[b * rows : (b + 1) * rows], dz=d).astype(F32)

    block = tile(width, 512)
    steps = width // block

    def whole(a):
        return pl.BlockSpec(a.shape, lambda j: (0, 0))

    parts = [s[0] for s in saved]
    small = [s[2] for s in saved] + [s[3] for s in saved] + [s[1] for s in saved]
    grad_gate, grad_up, grad_down = call(
        outer,
        [((share, width), BF)] * 3,
        parts + parts + small,
        2 * 3 * 4 * count * share * width,
        2 * (4 * count * full + 3 * share * width),
        grid=(steps,),
        in_specs=[pl.BlockSpec((p.shape[0], block), lambda j: (0, j)) for p in parts]
        + [pl.BlockSpec((p.shape[0], block), lambda j: (0, j + steps)) for p in parts]
        + [whole(a) for a in small],
        out_specs=[pl.BlockSpec((share, block), lambda j: (0, j))] * 3,
    )
    return (
        summed[:, :width].astype(BF),
        summed[:, width : width + top],
        grad_gate[None],
        grad_up[None],
        grad_down[None],
    )


def solution(mesh):
    both = P(("seq", "expert"), None)
    weight = P("expert", "seq", None)
    return jax.shard_map(
        body,
        mesh=mesh,
        in_specs=(both, both, both, both, weight, weight, weight),
        out_specs=(both, both, weight, weight, weight),
        check_vma=False,
    )
```

```python
import jax
import jax.numpy as jnp
from jax import lax
from jax.experimental import pallas as pl
from jax.experimental.pallas import tpu as pltpu
from jax.sharding import PartitionSpec as P

NY, NZ, NC = 4, 8, 2
Z_ORDER = (0, -1, 1, -2, 2, -3, 3, 4)
Y_ORDER = (0, 1, -1, 2)
CAP = 2
PAD = 128
BF = jnp.bfloat16
F32 = jnp.float32
COLS = (((1,), (1,)), ((), ()))
ROWS = (((0,), (0,)), ((), ()))
ANY = pl.BlockSpec(memory_space=pl.ANY)
VMEM = pl.BlockSpec(memory_space=pltpu.VMEM)
SMEM = pl.BlockSpec(memory_space=pltpu.SMEM)


def dot(a, b, dims=(((1,), (0,)), ((), ()))):
    return lax.dot_general(a, b, dims, preferred_element_type=F32)


def tile(n, most):
    return max(b for b in range(PAD, most + 1, PAD) if n % b == 0)


def call(kernel, outs, args, flops, moved, scratch=(), **more):
    specs = dict(
        in_specs=[SMEM if a.dtype == jnp.int32 else VMEM for a in args],
        out_specs=[VMEM] * len(outs),
        scratch_shapes=list(scratch),
    )
    specs.update(more)
    return pl.pallas_call(
        kernel,
        out_shape=[jax.ShapeDtypeStruct(s, d) for s, d in outs],
        compiler_params=pltpu.CompilerParams(vmem_limit_bytes=44 * 2**20),
        cost_estimate=pl.CostEstimate(flops=flops, bytes_accessed=moved, transcendentals=0),
        **specs,
    )(*args)


def after(v, *first):
    return pl.pallas_call(
        lambda *refs: None,
        out_shape=jax.ShapeDtypeStruct(v.shape, v.dtype),
        in_specs=[ANY] * (1 + len(first)),
        out_specs=ANY,
        input_output_aliases={0: 0},
    )(v, *first)


def move(v, dy=0, dz=0, dc=0):
    pairs = []
    for y in range(NY):
        for z in range(NZ):
            for c in range(NC):
                to = (((y + dy) % NY) * NZ + (z + dz) % NZ) * NC + (c + dc) % NC
                pairs.append(((y * NZ + z) * NC + c, to))
    return lax.ppermute(v, "expert", pairs)


def move_x(v, d):
    n = lax.axis_size("seq")
    return lax.ppermute(v, "seq", [(i, (i + d) % n) for i in range(n)])


def lanes(shape):
    return lax.broadcasted_iota(jnp.int32, shape, 1)


def one_hot(slot, slots):
    at = lanes(slot.shape)
    pick = jnp.zeros(slot.shape, F32)
    for d in range(NY):
        of = jnp.sum(jnp.where(at == d, slot, 0.0), axis=1, keepdims=True)
        pick = jnp.where(of == (at - d * slots).astype(F32), 1.0, pick)
    return pick.astype(BF)


def choose(rows, top, width, block, targets, mine, other, s0, s1, s2, s3, slot_out, ids_out):
    count = 2 * mine.shape[0]
    slots = s0.shape[0]
    tail = jnp.concatenate([mine[:, 2 * width :], other[:, 2 * width :]], axis=0).astype(F32)
    at = lanes(tail.shape)
    row = lax.broadcasted_iota(jnp.int32, tail.shape, 0)
    ids = jnp.where(at < top, tail, -1.0)
    chosen = jnp.zeros(tail.shape, F32)
    for d in range(NY):
        hit = jnp.where(ids == targets[d].astype(F32), 1.0, 0.0)
        chosen = jnp.where(at == d, jnp.max(hit, axis=1, keepdims=True), chosen)
    before = jnp.where((row // rows == at // rows) & (at < row), 1.0, 0.0).astype(BF)
    place = dot(before, chosen.astype(BF))
    slot = jnp.where(chosen > 0.0, place + (row // rows * CAP).astype(F32), -4.0 * PAD)
    slot_out[...] = slot
    ids_out[...] = ids
    pick = one_hot(slot, slots)
    top_half, low_half = pick[: count // 2], pick[count // 2 :]
    outs = (s0, s1, s2, s3)
    for j in range(0, mine.shape[1], block):
        part = dot(top_half, mine[:, j : j + block], ROWS)
        part = (part + dot(low_half, other[:, j : j + block], ROWS)).astype(BF)
        for d in range(NY):
            outs[d][:, j : j + block] = part[d * slots : (d + 1) * slots]


def expert(top, block, me, own, left, right, fa, fb, wg, wu, wd, part, r_own, r_left, r_right, r_far, hg, dg, du):
    n = own.shape[0]
    width = wg.shape[1]
    part[:n] = own[...]
    part[n : 2 * n] = left[...]
    part[2 * n : 3 * n] = right[...]
    part[3 * n : 3 * n + n // 2] = fa[...]
    part[3 * n + n // 2 :] = fb[...]
    tail = part[:, 2 * width :].astype(F32)
    gates = pltpu.roll(tail, PAD - top, 1)
    mask = (tail == me[0].astype(F32)) & (lanes(tail.shape) < top)
    gate = jnp.sum(jnp.where(mask, gates, 0.0), axis=1, keepdims=True)
    x = part[:, :width]
    pre_gate = dot(x, wg[...], COLS)
    pre_up = dot(x, wu[...], COLS)
    plain = dot(part[:, width : 2 * width], wd[...], COLS)
    sig = jax.nn.sigmoid(pre_gate)
    act = pre_gate * sig
    hidden = act * pre_up
    router = jnp.sum(hidden.astype(BF).astype(F32) * plain, axis=1, keepdims=True)
    grad_hidden = gate * plain
    d_gate = (grad_hidden * pre_up * (sig * (1.0 + pre_gate * (1.0 - sig)))).astype(BF)
    d_up = (grad_hidden * act).astype(BF)
    hg[...] = (gate * hidden).astype(BF)
    dg[...] = d_gate
    du[...] = d_up
    outs = (r_own, r_left, r_right, r_far)
    for j in range(0, width, block):
        back = dot(d_gate, wg[:, j : j + block]) + dot(d_up, wu[:, j : j + block])
        for i, out in enumerate(outs):
            out[:, j : j + block] = back[i * n : (i + 1) * n].astype(out.dtype)
    wide = jnp.broadcast_to(router, (4 * n, PAD))
    for i, out in enumerate(outs):
        out[:, width:] = wide[i * n : (i + 1) * n].astype(out.dtype)


def combine(width, block, targets, slot, ids, h0, h1, h2, h3, keep, send, home):
    slots = h0.shape[0]
    half = keep.shape[0]
    for d, h in enumerate((h0, h1, h2, h3)):
        home[d * slots : (d + 1) * slots] = h[...]
    pick = one_hot(slot[...], slots)
    for j in range(0, width, block):
        part = dot(pick, home[:, j : j + block])
        keep[:, j : j + block] = part[:half]
        send[:, j : j + block] = part[half:].astype(BF)
    at = lanes(pick.shape)
    routed = jnp.zeros(slot.shape, F32)
    for d in range(NY):
        val = dot(jnp.where(at // slots == d, pick, jnp.zeros_like(pick)), home[:, width:])
        routed = routed + jnp.where(ids[...] == targets[d].astype(F32), val, 0.0)
    keep[:, width:] = routed[:half]
    send[:, width:] = routed[half:].astype(BF)


def outer(xa, xb, xc, ya, yb, yc, ga, gb, gc, ua, ub, uc, ha, hb, hc, o_gate, o_up, o_down):
    xs = (xa[...], xb[...], xc[...])
    ys = (ya[...], yb[...], yc[...])
    o_gate[...] = sum(dot(d[...], x, ROWS) for d, x in zip((ga, gb, gc), xs)).astype(BF)
    o_up[...] = sum(dot(d[...], x, ROWS) for d, x in zip((ua, ub, uc), xs)).astype(BF)
    o_down[...] = sum(dot(h[...], y, ROWS) for h, y in zip((ha, hb, hc), ys)).astype(BF)


def body(tokens, out_grad, expert_ids, gate_values, gate_weight, up_weight, down_weight):
    rows, width = tokens.shape
    top = expert_ids.shape[1]
    share = gate_weight.shape[1]
    full, back_w = 2 * width + PAD, width + PAD
    me = lax.axis_index("expert").astype(jnp.int32)
    my_y, my_zc = me // (NZ * NC), me % (NZ * NC)
    targets = jnp.stack([((my_y + d) % NY) * (NZ * NC) + my_zc for d in Y_ORDER])
    me = me[None]
    wg, wu, wd = gate_weight[0], up_weight[0], down_weight[0]

    extra = jnp.concatenate(
        [expert_ids.astype(BF), gate_values, jnp.zeros((rows, PAD - 2 * top), BF)], axis=1
    )
    pay = jnp.concatenate([tokens, out_grad, extra], axis=1)

    have = {0: pay}
    for d in (-2, 2, -1, 1):
        have[d] = move(pay, dz=-d)
    far_z = [move(have[-2][:, :width], dz=2), move(have[2][:, width:], dz=-2)]
    have[-3], have[3] = move(have[-2], dz=1), move(have[2], dz=-1)
    have[NZ // 2] = jnp.concatenate(far_z, axis=1)
    mine = jnp.concatenate([have[d] for d in Z_ORDER], axis=0)
    other = move(mine, dc=1)
    count = 2 * rows * NZ
    slots = count // rows * CAP

    def choose_k(*refs):
        choose(rows, top, width, tile(full, 1664), *refs)

    s0, s1, s2, s3, slot, ids = call(
        choose_k,
        [((slots, full), BF)] * NY + [((count, PAD), F32)] * 2,
        (targets, mine, other),
        2 * count * NY * slots * full,
        2 * count * full * 2,
    )
    def expert_k(*refs):
        expert(top, tile(width, 1024), *refs)

    def both(v):
        return move_x(v, 1), move_x(v, -1)

    def onward(near):
        n = near[0].shape[0] // 2
        return move_x(near[0][:n], 1), move_x(near[1][n:], -1)

    def back_and_forth(own, near, far, *first):
        n = own.shape[0]
        part, r_own, r_left, r_right, r_far, hg, dg, du = call(
            expert_k,
            [((4 * n, full), BF), ((n, back_w), F32)]
            + [((n, back_w), BF)] * 3
            + [((4 * n, share), BF)] * 3,
            (after(me, *first) if first else me, own, *near, *far, wg, wu, wd),
            2 * 4 * n * width * share * 5,
            2 * (8 * n * full + 4 * n * back_w + 3 * share * width),
        )
        return (part, dg, du, hg), r_own, (move_x(r_far, 2), move_x(r_left, -1), move_x(r_right, 1))

    near0 = both(s0)
    ring = jnp.concatenate([move(s1, dy=1), move(s2, dy=-1)], axis=0)
    ring = after(ring, *near0)
    far0 = onward(near0)
    near1 = both(ring)
    across = move(after(s3, *far0), dy=2)
    saved0, own0, got0 = back_and_forth(s0, near0, far0)
    across = after(across, *near1, own0)
    far1 = onward(near1)
    near2 = both(across)
    saved1, own1, got1 = back_and_forth(ring, near1, far1, *got0)
    far2 = onward(near2)
    saved2, own2, got2 = back_and_forth(across, near2, far2, own1)
    saved2 = (saved2[0], after(saved2[1], *got1), *saved2[2:])

    block = tile(width, 512)
    steps = width // block

    def whole(a):
        return pl.BlockSpec(a.shape, lambda j: (0, 0))

    parts, *small = zip(saved0, saved1, saved2)
    parts, small = list(parts), [a for group in small for a in group]
    grad_gate, grad_up, grad_down = call(
        outer,
        [((share, width), BF)] * 3,
        parts + parts + small,
        2 * 3 * 4 * count * share * width,
        2 * (4 * count * full + 3 * share * width),
        grid=(steps,),
        in_specs=[pl.BlockSpec((p.shape[0], block), lambda j: (0, j)) for p in parts]
        + [pl.BlockSpec((p.shape[0], block), lambda j: (0, j + steps)) for p in parts]
        + [whole(a) for a in small],
        out_specs=[pl.BlockSpec((share, block), lambda j: (0, j))] * 3,
    )
    own2 = after(own2, grad_down)
    returned = [
        (o + a.astype(F32) + b.astype(F32) + c.astype(F32)).astype(BF)
        for o, (a, b, c) in ((own0, got0), (own1, got1), (own2, got2))
    ]

    def combine_k(*refs):
        combine(width, tile(width, 1024), *refs)

    keep, send = call(
        combine_k,
        [((count // NC, back_w), F32), ((count // NC, back_w), BF)],
        (
            targets,
            slot,
            ids,
            returned[0],
            move(returned[1][:slots], dy=-1),
            move(returned[1][slots:], dy=1),
            move(returned[2], dy=2),
        ),
        2 * count * count * back_w,
        10 * count * back_w // 2,
        scratch=[pltpu.VMEM((count, back_w), BF)],
    )
    cored = keep + move(send, dc=1).astype(F32)
    sent = cored.astype(BF)
    summed = cored[:rows]
    for b, d in enumerate(Z_ORDER):
        if d:
            summed = summed + move(sent[b * rows : (b + 1) * rows], dz=d).astype(F32)

    return (
        summed[:, :width].astype(BF),
        summed[:, width : width + top],
        grad_gate[None],
        grad_up[None],
        grad_down[None],
    )


def solution(mesh):
    both = P(("seq", "expert"), None)
    weight = P("expert", "seq", None)
    return jax.shard_map(
        body,
        mesh=mesh,
        in_specs=(both, both, both, both, weight, weight, weight),
        out_specs=(both, both, weight, weight, weight),
        check_vma=False,
    )
```

```python
import jax
import jax.numpy as jnp
from jax import lax
from jax.experimental import pallas as pl
from jax.experimental.pallas import tpu as pltpu
from jax.sharding import PartitionSpec as P

NY, NZ, NC = 4, 8, 2
EARLY = (0, -1, 1, 2)
LATE = (-2, -3, 3, 4)
Y_ORDER = (0, 1, -1, 2)
CAP = 2
PAD = 128
BF = jnp.bfloat16
F32 = jnp.float32
COLS = (((1,), (1,)), ((), ()))
ROWS = (((0,), (0,)), ((), ()))
ANY = pl.BlockSpec(memory_space=pl.ANY)
VMEM = pl.BlockSpec(memory_space=pltpu.VMEM)
SMEM = pl.BlockSpec(memory_space=pltpu.SMEM)


def dot(a, b, dims=(((1,), (0,)), ((), ()))):
    return lax.dot_general(a, b, dims, preferred_element_type=F32)


def tile(n, most):
    return max(b for b in range(PAD, most + 1, PAD) if n % b == 0)


def call(kernel, outs, args, flops, moved, first=(), mib=32, **more):
    specs = dict(
        in_specs=[SMEM if a.dtype == jnp.int32 else VMEM for a in args],
        out_specs=[VMEM] * len(outs),
    )
    specs.update(more)
    specs["in_specs"] = list(specs["in_specs"]) + [ANY] * len(first)
    count = len(args)

    def without(*refs):
        kernel(*refs[:count], *refs[count + len(first) :])

    return pl.pallas_call(
        without,
        out_shape=[jax.ShapeDtypeStruct(s, d) for s, d in outs],
        compiler_params=pltpu.CompilerParams(vmem_limit_bytes=mib * 2**20),
        cost_estimate=pl.CostEstimate(flops=flops, bytes_accessed=moved, transcendentals=0),
        **specs,
    )(*args, *first)


def move(v, dy=0, dz=0, dc=0):
    pairs = []
    for y in range(NY):
        for z in range(NZ):
            for c in range(NC):
                to = (((y + dy) % NY) * NZ + (z + dz) % NZ) * NC + (c + dc) % NC
                pairs.append(((y * NZ + z) * NC + c, to))
    return lax.ppermute(v, "expert", pairs)


def move_x(v, d):
    n = lax.axis_size("seq")
    return lax.ppermute(v, "seq", [(i, (i + d) % n) for i in range(n)])


def lanes(shape):
    return lax.broadcasted_iota(jnp.int32, shape, 1)


def one_hot(slot, slots):
    at = lanes(slot.shape)
    pick = jnp.zeros(slot.shape, F32)
    for d in range(NY):
        of = jnp.sum(jnp.where(at == d, slot, 0.0), axis=1, keepdims=True)
        pick = jnp.where(of == (at - d * slots).astype(F32), 1.0, pick)
    return pick.astype(BF)


def stacked(refs, cols):
    return jnp.concatenate([r[:, cols] for r in refs], axis=0) if len(refs) > 1 else refs[0][:, cols]


def choose(rows, top, width, block, groups, targets, *refs):
    *pieces, s0, s1, s2, s3, slot_out, ids_out = refs
    outs = (s0, s1, s2, s3)
    slots = s0.shape[0] // len(groups)
    for g, many in enumerate(groups):
        mine, pieces = pieces[:many], pieces[many:]
        tail = stacked(mine, slice(2 * width, 2 * width + PAD)).astype(F32)
        count = tail.shape[0]
        at = lanes(tail.shape)
        row = lax.broadcasted_iota(jnp.int32, tail.shape, 0)
        ids = jnp.where(at < top, tail, -1.0)
        chosen = jnp.zeros(tail.shape, F32)
        for d in range(NY):
            hit = jnp.where(ids == targets[d].astype(F32), 1.0, 0.0)
            chosen = jnp.where(at == d, jnp.max(hit, axis=1, keepdims=True), chosen)
        r_at = lax.broadcasted_iota(jnp.int32, (count, count), 0)
        c_at = lanes((count, count))
        before = jnp.where((r_at // rows == c_at // rows) & (c_at < r_at), 1.0, 0.0).astype(BF)
        place = dot(before, chosen.astype(BF))
        slot = jnp.where(chosen > 0.0, place + (row // rows * CAP).astype(F32), -4.0 * PAD)
        if g == 0:
            slot_out[...] = slot
            ids_out[...] = ids
        pick = one_hot(slot, slots)
        for j in range(0, 2 * width + PAD, block):
            part = dot(pick, stacked(mine, slice(j, j + block)), ROWS).astype(BF)
            for d in range(NY):
                outs[d][g * slots : (g + 1) * slots, j : j + block] = part[d * slots : (d + 1) * slots]


def expert(top, block, per_x, me, *refs):
    *pieces, wg, wu, wd, r_own, r_left, r_right, r_far, hg, dg, du = refs
    width = wg.shape[1]
    tail = stacked(pieces, slice(2 * width, 2 * width + PAD)).astype(F32)
    gates = pltpu.roll(tail, PAD - top, 1)
    mask = (tail == me[0].astype(F32)) & (lanes(tail.shape) < top)
    gate = jnp.sum(jnp.where(mask, gates, 0.0), axis=1, keepdims=True)
    x = stacked(pieces, slice(0, width))
    pre_gate = dot(x, wg[...], COLS)
    pre_up = dot(x, wu[...], COLS)
    plain = dot(stacked(pieces, slice(width, 2 * width)), wd[...], COLS)
    sig = jax.nn.sigmoid(pre_gate)
    act = pre_gate * sig
    hidden = act * pre_up
    router = jnp.sum(hidden.astype(BF).astype(F32) * plain, axis=1, keepdims=True)
    grad_hidden = gate * plain
    d_gate = (grad_hidden * pre_up * (sig * (1.0 + pre_gate * (1.0 - sig)))).astype(BF)
    d_up = (grad_hidden * act).astype(BF)
    hg[...] = (gate * hidden).astype(BF)
    dg[...] = d_gate
    du[...] = d_up
    outs = (r_own, r_left, r_right, r_far)

    def put(cols, v):
        for out, spans in zip(outs, per_x):
            at = 0
            for start, n in spans:
                out[at : at + n, cols] = v[start : start + n].astype(out.dtype)
                at += n

    for j in range(0, width, block):
        cols = slice(j, j + block)
        put(cols, dot(d_gate, wg[:, cols]) + dot(d_up, wu[:, cols]))
    put(slice(width, width + PAD), jnp.broadcast_to(router, (router.shape[0], PAD)))


def add_up(o_late, o_far, l1, l2, l3, f1, f2, f3, own, up, down, across):
    slots = own.shape[0]
    late = o_late[...] + l1[...].astype(F32) + l2[...].astype(F32) + l3[...].astype(F32)
    far = o_far[...] + f1[...].astype(F32) + f2[...].astype(F32) + f3[...].astype(F32)
    late = late.astype(BF)
    own[...] = late[:slots]
    up[...] = late[slots : 2 * slots]
    down[...] = late[2 * slots : 3 * slots]
    across[:slots] = far.astype(BF)
    across[slots:] = late[3 * slots :]


def combine(width, block, targets, slot_e, ids_e, slot_l, ids_l, e0, e1, e2, l0, l1, l2, far, keep, send):
    slots = l0.shape[0]
    half = keep.shape[0] // 2
    for g, (slot, ids, home) in enumerate(
        ((slot_e, ids_e, (e0, e1, e2, far)), (slot_l, ids_l, (l0, l1, l2, far)))
    ):
        def block_of(cols):
            last = home[3][g * slots : (g + 1) * slots, cols]
            return jnp.concatenate([h[:slots, cols] for h in home[:3]] + [last], axis=0)

        pick = one_hot(slot[...], slots)
        narrow = pick[:, : NY * slots]
        rows = slice(g * half, (g + 1) * half)
        for j in range(0, width, block):
            cols = slice(j, j + block)
            part = dot(narrow, block_of(cols))
            keep[rows, cols] = part[:half]
            send[rows, cols] = part[half:].astype(BF)
        tail = block_of(slice(width, width + PAD))
        at = lanes(narrow.shape)
        routed = jnp.zeros(slot.shape, F32)
        for d in range(NY):
            val = dot(jnp.where(at // slots == d, narrow, jnp.zeros_like(narrow)), tail)
            routed = routed + jnp.where(ids[...] == targets[d].astype(F32), val, 0.0)
        keep[rows, width:] = routed[:half]
        send[rows, width:] = routed[half:].astype(BF)


def outer(many, *refs):
    xs, ys = refs[:many], refs[many : 2 * many]
    *small, o_gate, o_up, o_down = refs[2 * many :]
    third = len(small) // 3
    every = slice(None)
    x, y = stacked(xs, every), stacked(ys, every)
    o_gate[...] = dot(stacked(small[:third], every), x, ROWS).astype(BF)
    o_up[...] = dot(stacked(small[third : 2 * third], every), x, ROWS).astype(BF)
    o_down[...] = dot(stacked(small[2 * third :], every), y, ROWS).astype(BF)


def body(tokens, out_grad, expert_ids, gate_values, gate_weight, up_weight, down_weight):
    rows, width = tokens.shape
    top = expert_ids.shape[1]
    share = gate_weight.shape[1]
    full, back_w = 2 * width + PAD, width + PAD
    me = lax.axis_index("expert").astype(jnp.int32)
    my_y, my_zc = me // (NZ * NC), me % (NZ * NC)
    targets = jnp.stack([((my_y + d) % NY) * (NZ * NC) + my_zc for d in Y_ORDER])
    me = me[None]
    wg, wu, wd = gate_weight[0], up_weight[0], down_weight[0]

    extra = jnp.concatenate(
        [expert_ids.astype(BF), gate_values, jnp.zeros((rows, PAD - 2 * top), BF)], axis=1
    )
    pay = jnp.concatenate([tokens, out_grad, extra], axis=1)

    def both(v):
        return move_x(v, 1), move_x(v, -1)

    def onward(near):
        n = near[0].shape[0] // 2
        return move_x(near[0][:n], 1), move_x(near[1][n:], -1)

    have = {0: pay}
    for d in (1, -1, 2, -2):
        have[d] = move(pay, dz=-d)
    early = jnp.concatenate([have[d] for d in EARLY], axis=0)
    early_near = both(early)
    far_z = [move(have[-2][:, :width], dz=2), move(have[2][:, width:], dz=-2)]
    have[-3], have[3] = move(have[-2], dz=1), move(have[2], dz=-1)
    have[NZ // 2] = jnp.concatenate(far_z, axis=1)
    late = jnp.concatenate([have[d] for d in LATE], axis=0)
    early_far = onward(early_near)
    held = rows * len(EARLY)
    count = NC * held
    slots = count // rows * CAP

    def choosing(groups, pieces, first=()):
        def kernel(*refs):
            choose(rows, top, width, tile(full, 1664), groups, *refs)

        return call(
            kernel,
            [((slots * len(groups), full), BF)] * NY + [((count, PAD), F32)] * 2,
            (targets, *pieces),
            2 * count * PAD * full * len(groups),
            4 * count * full * len(groups),
            first,
        )

    l0, l1, l2, l3, slot_l, ids_l = choosing((2,), (late, move(late, dc=1)))
    late = jnp.concatenate([l0, move(l1, dy=1), move(l2, dy=-1), move(l3, dy=2)], axis=0)
    late_near = both(late)

    pieces = []
    for piece in ((early,), early_near[:1], early_near[1:], early_far):
        pieces += [*piece, *(move(p, dc=1) for p in piece)]
    e0, e1, e2, e3, slot_e, ids_e = choosing((2, 2, 2, 4), pieces, (late,))
    e1, e2, e3 = move(e1, dy=1), move(e2, dy=-1), move(e3, dy=2)
    late_far = onward(late_near)

    def back_and_forth(parts, per_x, first=()):
        def kernel(*refs):
            expert(top, tile(width, 1024), per_x, *refs)

        n = sum(p.shape[0] for p in parts)
        r_own, r_left, r_right, r_far, hg, dg, du = call(
            kernel,
            [((n // 4, back_w), F32)] + [((n // 4, back_w), BF)] * 3 + [((n, share), BF)] * 3,
            (me, *parts, wg, wu, wd),
            2 * n * width * share * 5,
            2 * (n * full + n * back_w + 3 * share * width),
            first,
        )
        return (dg, du, hg), r_own, (move_x(r_far, 2), move_x(r_left, -1), move_x(r_right, 1))

    def spans(many, n):
        return [[(i * 4 * n + x * n, n) for i in range(many)] for x in range(4)]

    late_parts = [late, *late_near, *late_far]
    small0, own0, got0 = back_and_forth([e0, e1, e2], spans(3, slots), late_near)
    small1, own1, got1 = back_and_forth(late_parts, spans(1, NY * slots))
    small2, own2, got2 = back_and_forth([e3], spans(1, slots), got0)

    block = tile(width, 512)
    steps = width // block
    parts = [e0, e1, e2, *late_parts, e3]
    small = [a for group in zip(small0, small1, small2) for a in group]

    def outer_k(*refs):
        outer(len(parts), *refs)

    grad_gate, grad_up, grad_down = call(
        outer_k,
        [((share, width), BF)] * 3,
        parts + parts + small,
        2 * 3 * 8 * count * share * width,
        2 * (8 * count * full + 3 * share * width),
        got1,
        grid=(steps,),
        in_specs=[pl.BlockSpec((p.shape[0], block), lambda j: (0, j)) for p in parts]
        + [pl.BlockSpec((p.shape[0], block), lambda j: (0, j + steps)) for p in parts]
        + [pl.BlockSpec(a.shape, lambda j: (0, 0)) for a in small],
        out_specs=[pl.BlockSpec((share, block), lambda j: (0, j))] * 3,
    )

    total = (own0 + sum(g.astype(F32) for g in got0)).astype(BF)
    e1, e2 = move(total[slots : 2 * slots], dy=-1), move(total[2 * slots :], dy=1)
    l0, l1, l2, far = call(
        add_up,
        [((slots, back_w), BF)] * 3 + [((2 * slots, back_w), BF)],
        (own1, own2, *got1, *got2),
        0,
        20 * count * back_w,
        (grad_down,),
    )

    def combine_k(*refs):
        combine(width, tile(width, 1024), *refs)

    keep, send = call(
        combine_k,
        [((count, back_w), F32), ((count, back_w), BF)],
        (targets, slot_e, ids_e, slot_l, ids_l, total, e1, e2, l0)
        + (move(l1, dy=-1), move(l2, dy=1), move(far, dy=2)),
        4 * count * count * back_w,
        10 * count * back_w,
    )
    cored = keep + move(send, dc=1).astype(F32)
    sent = cored.astype(BF)
    summed = cored[:rows]
    for b, d in enumerate(EARLY + LATE):
        if d:
            summed = summed + move(sent[b * rows : (b + 1) * rows], dz=d).astype(F32)
    return (
        summed[:, :width].astype(BF),
        summed[:, width : width + top],
        grad_gate[None],
        grad_up[None],
        grad_down[None],
    )


def solution(mesh):
    both = P(("seq", "expert"), None)
    weight = P("expert", "seq", None)
    return jax.shard_map(
        body,
        mesh=mesh,
        in_specs=(both, both, both, both, weight, weight, weight),
        out_specs=(both, both, weight, weight, weight),
        check_vma=False,
    )
```

```python
import jax
import jax.numpy as jnp
from jax import lax
from jax.experimental import pallas as pl
from jax.experimental.pallas import tpu as pltpu
from jax.sharding import PartitionSpec as P

NY, NZ, NC = 4, 8, 2
EARLY = (0, -1, 1, 2)
LATE = (-2, -3, 3, 4)
Y_ORDER = (0, 1, -1, 2)
CAP = 2
PAD = 128
BF = jnp.bfloat16
F32 = jnp.float32
COLS = (((1,), (1,)), ((), ()))
ROWS = (((0,), (0,)), ((), ()))
ANY = pl.BlockSpec(memory_space=pl.ANY)
VMEM = pl.BlockSpec(memory_space=pltpu.VMEM)
SMEM = pl.BlockSpec(memory_space=pltpu.SMEM)


def dot(a, b, dims=(((1,), (0,)), ((), ()))):
    return lax.dot_general(a, b, dims, preferred_element_type=F32)


def tile(n, most):
    return max(b for b in range(PAD, most + 1, PAD) if n % b == 0)


def call(kernel, outs, args, flops, moved, first=(), mib=32, **more):
    specs = dict(
        in_specs=[SMEM if a.dtype == jnp.int32 else VMEM for a in args],
        out_specs=[VMEM] * len(outs),
    )
    specs.update(more)
    specs["in_specs"] = list(specs["in_specs"]) + [ANY] * len(first)
    count = len(args)

    def without(*refs):
        kernel(*refs[:count], *refs[count + len(first) :])

    return pl.pallas_call(
        without,
        out_shape=[jax.ShapeDtypeStruct(s, d) for s, d in outs],
        compiler_params=pltpu.CompilerParams(vmem_limit_bytes=mib * 2**20),
        cost_estimate=pl.CostEstimate(flops=flops, bytes_accessed=moved, transcendentals=0),
        **specs,
    )(*args, *first)


def move(v, dy=0, dz=0, dc=0):
    pairs = []
    for y in range(NY):
        for z in range(NZ):
            for c in range(NC):
                to = (((y + dy) % NY) * NZ + (z + dz) % NZ) * NC + (c + dc) % NC
                pairs.append(((y * NZ + z) * NC + c, to))
    return lax.ppermute(v, "expert", pairs)


def move_x(v, d):
    n = lax.axis_size("seq")
    return lax.ppermute(v, "seq", [(i, (i + d) % n) for i in range(n)])


def lanes(shape):
    return lax.broadcasted_iota(jnp.int32, shape, 1)


def one_hot(slot, slots):
    at = lanes(slot.shape)
    pick = jnp.zeros(slot.shape, F32)
    for d in range(NY):
        of = jnp.sum(jnp.where(at == d, slot, 0.0), axis=1, keepdims=True)
        pick = jnp.where(of == (at - d * slots).astype(F32), 1.0, pick)
    return pick.astype(BF)


def stacked(refs, cols):
    return jnp.concatenate([r[:, cols] for r in refs], axis=0) if len(refs) > 1 else refs[0][:, cols]


def choose(rows, top, width, block, groups, slots, into, targets, *refs):
    pieces, outs = refs[: sum(groups)], refs[sum(groups) : -2]
    slot_out, ids_out = refs[-2:]
    for g, many in enumerate(groups):
        mine, pieces = pieces[:many], pieces[many:]
        tail = stacked(mine, slice(2 * width, 2 * width + PAD)).astype(F32)
        count = tail.shape[0]
        at = lanes(tail.shape)
        row = lax.broadcasted_iota(jnp.int32, tail.shape, 0)
        ids = jnp.where(at < top, tail, -1.0)
        chosen = jnp.zeros(tail.shape, F32)
        for d in range(NY):
            hit = jnp.where(ids == targets[d].astype(F32), 1.0, 0.0)
            chosen = jnp.where(at == d, jnp.max(hit, axis=1, keepdims=True), chosen)
        r_at = lax.broadcasted_iota(jnp.int32, (count, count), 0)
        c_at = lanes((count, count))
        before = jnp.where((r_at // rows == c_at // rows) & (c_at < r_at), 1.0, 0.0).astype(BF)
        place = dot(before, chosen.astype(BF))
        slot = jnp.where(chosen > 0.0, place + (row // rows * CAP).astype(F32), -4.0 * PAD)
        if g == 0:
            slot_out[...] = slot
            ids_out[...] = ids
        pick = one_hot(slot, slots)
        for j in range(0, 2 * width + PAD, block):
            part = dot(pick, stacked(mine, slice(j, j + block)), ROWS).astype(BF)
            for d in range(NY):
                out, at = into[g][d]
                outs[out][at : at + slots, j : j + block] = part[d * slots : (d + 1) * slots]


def expert(top, block, per_x, sizes, me, *refs):
    *pieces, wg, wu, wd, r_own, r_left, r_right, r_far, hg, dg, du = refs
    pieces = [p.at[:n] for p, n in zip(pieces, sizes)]
    width = wg.shape[1]
    tail = stacked(pieces, slice(2 * width, 2 * width + PAD)).astype(F32)
    gates = pltpu.roll(tail, PAD - top, 1)
    mask = (tail == me[0].astype(F32)) & (lanes(tail.shape) < top)
    gate = jnp.sum(jnp.where(mask, gates, 0.0), axis=1, keepdims=True)
    x = stacked(pieces, slice(0, width))
    pre_gate = dot(x, wg[...], COLS)
    pre_up = dot(x, wu[...], COLS)
    plain = dot(stacked(pieces, slice(width, 2 * width)), wd[...], COLS)
    sig = jax.nn.sigmoid(pre_gate)
    act = pre_gate * sig
    hidden = act * pre_up
    router = jnp.sum(hidden.astype(BF).astype(F32) * plain, axis=1, keepdims=True)
    grad_hidden = gate * plain
    d_gate = (grad_hidden * pre_up * (sig * (1.0 + pre_gate * (1.0 - sig)))).astype(BF)
    d_up = (grad_hidden * act).astype(BF)
    hg[...] = (gate * hidden).astype(BF)
    dg[...] = d_gate
    du[...] = d_up
    outs = (r_own, r_left, r_right, r_far)

    def put(cols, v):
        for out, spans in zip(outs, per_x):
            at = 0
            for start, n in spans:
                out[at : at + n, cols] = v[start : start + n].astype(out.dtype)
                at += n

    for j in range(0, width, block):
        cols = slice(j, j + block)
        put(cols, dot(d_gate, wg[:, cols]) + dot(d_up, wu[:, cols]))
    put(slice(width, width + PAD), jnp.broadcast_to(router, (router.shape[0], PAD)))


def add_up(mine, a, b, c, *outs):
    total = mine[...] + a[...].astype(F32) + b[...].astype(F32) + c[...].astype(F32)
    slots = outs[0].shape[0]
    for d, out in enumerate(outs):
        out[...] = total[d * slots : (d + 1) * slots].astype(BF)


def combine(width, block, targets, slot_e, ids_e, slot_l, ids_l, e0, e1, e2, e3, l0, l1, l2, l3, keep, send):
    slots = l0.shape[0]
    half = keep.shape[0] // 2
    for g, (slot, ids, home) in enumerate(
        ((slot_e, ids_e, (e0, e1, e2, e3)), (slot_l, ids_l, (l0, l1, l2, l3)))
    ):
        pick = one_hot(slot[...], slots)
        narrow = pick[:, : NY * slots]
        rows = slice(g * half, (g + 1) * half)
        for j in range(0, width, block):
            cols = slice(j, j + block)
            part = dot(narrow, stacked(home, cols))
            keep[rows, cols] = part[:half]
            send[rows, cols] = part[half:].astype(BF)
        tail = stacked(home, slice(width, width + PAD))
        at = lanes(narrow.shape)
        routed = jnp.zeros(slot.shape, F32)
        for d in range(NY):
            val = dot(jnp.where(at // slots == d, narrow, jnp.zeros_like(narrow)), tail)
            routed = routed + jnp.where(ids[...] == targets[d].astype(F32), val, 0.0)
        keep[rows, width:] = routed[:half]
        send[rows, width:] = routed[half:].astype(BF)


def outer(many, *refs):
    xs, ys = refs[:many], refs[many : 2 * many]
    *small, o_gate, o_up, o_down = refs[2 * many :]
    third = len(small) // 3
    every = slice(None)
    x, y = stacked(xs, every), stacked(ys, every)
    o_gate[...] = dot(stacked(small[:third], every), x, ROWS).astype(BF)
    o_up[...] = dot(stacked(small[third : 2 * third], every), x, ROWS).astype(BF)
    o_down[...] = dot(stacked(small[2 * third :], every), y, ROWS).astype(BF)


def body(tokens, out_grad, expert_ids, gate_values, gate_weight, up_weight, down_weight):
    rows, width = tokens.shape
    top = expert_ids.shape[1]
    share = gate_weight.shape[1]
    full, back_w = 2 * width + PAD, width + PAD
    me = lax.axis_index("expert").astype(jnp.int32)
    my_y, my_zc = me // (NZ * NC), me % (NZ * NC)
    targets = jnp.stack([((my_y + d) % NY) * (NZ * NC) + my_zc for d in Y_ORDER])
    me = me[None]
    wg, wu, wd = gate_weight[0], up_weight[0], down_weight[0]

    extra = jnp.concatenate(
        [expert_ids.astype(BF), gate_values, jnp.zeros((rows, PAD - 2 * top), BF)], axis=1
    )
    pay = jnp.concatenate([tokens, out_grad, extra], axis=1)

    def both(v):
        return move_x(v, 1), move_x(v, -1)

    def onward(near):
        n = near[0].shape[0] // 2
        return move_x(near[0][:n], 1), move_x(near[1][n:], -1)

    have = {0: pay}
    for d in (1, -1, 2, -2):
        have[d] = move(pay, dz=-d)
    early = jnp.concatenate([have[d] for d in EARLY], axis=0)
    early_near = both(early)
    far_z = [move(have[-2][:, :width], dz=2), move(have[2][:, width:], dz=-2)]
    have[-3], have[3] = move(have[-2], dz=1), move(have[2], dz=-1)
    have[NZ // 2] = jnp.concatenate(far_z, axis=1)
    late = jnp.concatenate([have[d] for d in LATE], axis=0)
    early_far = onward(early_near)
    held = rows * len(EARLY)
    count = NC * held
    slots = count // rows * CAP

    def choosing(groups, into, outs, pieces, first=()):
        def kernel(*refs):
            choose(rows, top, width, tile(full, 1664), groups, slots, into, *refs)

        return call(
            kernel,
            [((n, full), BF) for n in outs] + [((count, PAD), F32)] * 2,
            (targets, *pieces),
            2 * count * PAD * full * len(groups),
            4 * count * full * len(groups),
            first,
        )

    early_groups = ((early,), early_near[:1], early_near[1:], early_far)
    crossed = [[move(p, dc=1) for p in group] for group in early_groups]
    l0, l1, l2, l3, slot_l, ids_l = choosing(
        (2,),
        [[(d, 0) for d in range(NY)]],
        [slots] * NY,
        (late, move(late, dc=1)),
        [p for group in crossed[:3] for p in group],
    )

    def join(*refs):
        *ins, out = refs
        for i, piece in enumerate(ins):
            out[i * slots : (i + 1) * slots] = piece[...]

    (late,) = call(
        join,
        [((NY * slots, full), BF)],
        (l0, move(l1, dy=1), move(l2, dy=-1), move(l3, dy=2)),
        0,
        16 * slots * full,
        crossed[3],
    )
    late_near = both(late)
    all_x, part_x = 4 * slots, 2 * slots
    into = [
        [(0, x * slots), (1, x * slots), (2, x * slots), (1 + x // 2, all_x + x % 2 * slots)]
        for x in range(4)
    ]
    pieces = [p for own, over in zip(early_groups, crossed) for p in (*own, *over)]
    e0, e1, e2, slot_e, ids_e = choosing(
        (2, 2, 2, 4), into, [all_x, all_x + part_x, all_x + part_x], pieces
    )
    e1, e2 = move(e1, dy=1), move(e2, dy=-1)
    early_parts = [e0, e1, e2, move(e1[all_x:], dy=1), move(e2[all_x:], dy=-1)]
    early_sizes = [all_x] * 3 + [part_x] * 2
    late_far = onward(late_near)

    def back_and_forth(parts, sizes, per_x, first=()):
        def kernel(*refs):
            expert(top, tile(width, 1024), per_x, sizes, *refs)

        n = sum(sizes)
        r_own, r_left, r_right, r_far, hg, dg, du = call(
            kernel,
            [((n // 4, back_w), F32)] + [((n // 4, back_w), BF)] * 3 + [((n, share), BF)] * 3,
            (me, *parts, wg, wu, wd),
            2 * n * width * share * 5,
            2 * (n * full + n * back_w + 3 * share * width),
            first,
        )
        return (dg, du, hg), r_own, (move_x(r_far, 2), move_x(r_left, -1), move_x(r_right, 1))

    def spans(many, n):
        return [[(i * 4 * n + x * n, n) for i in range(many)] for x in range(4)]

    late_parts = [late, *late_near, *late_far]
    late_sizes = [p.shape[0] for p in late_parts]
    small_l, own_l, got_l = back_and_forth(late_parts, late_sizes, spans(1, NY * slots))
    small_e, own_e, got_e = back_and_forth(early_parts, early_sizes, spans(NY, slots), (own_l,))

    block = tile(width, 512)
    steps = width // block
    parts = [*late_parts, *early_parts]
    sizes = late_sizes + early_sizes
    small = [a for group in zip(small_l, small_e) for a in group]

    def outer_k(*refs):
        outer(len(parts), *refs)

    grad_gate, grad_up, grad_down = call(
        outer_k,
        [((share, width), BF)] * 3,
        parts + parts + small,
        2 * 3 * 8 * count * share * width,
        2 * (8 * count * full + 3 * share * width),
        got_l,
        grid=(steps,),
        in_specs=[pl.BlockSpec((n, block), lambda j: (0, j)) for n in sizes]
        + [pl.BlockSpec((n, block), lambda j: (0, j + steps)) for n in sizes]
        + [pl.BlockSpec(a.shape, lambda j: (0, 0)) for a in small],
        out_specs=[pl.BlockSpec((share, block), lambda j: (0, j))] * 3,
    )

    def home(own, got, first):
        h0, h1, h2, h3 = call(
            add_up,
            [((slots, back_w), BF)] * NY,
            (own, *got),
            0,
            20 * count * back_w,
            first,
        )
        return h0, move(h1, dy=-1), move(h2, dy=1), move(h3, dy=2)

    home_l = home(own_l, got_l, ())
    home_e = home(own_e, got_e, (grad_down,))

    def combine_k(*refs):
        combine(width, tile(width, 1024), *refs)

    keep, send = call(
        combine_k,
        [((count, back_w), F32), ((count, back_w), BF)],
        (targets, slot_e, ids_e, slot_l, ids_l, *home_e, *home_l),
        4 * count * count * back_w,
        10 * count * back_w,
    )
    cored = keep + move(send, dc=1).astype(F32)
    sent = cored.astype(BF)
    summed = cored[:rows]
    for b, d in enumerate(EARLY + LATE):
        if d:
            summed = summed + move(sent[b * rows : (b + 1) * rows], dz=d).astype(F32)
    return (
        summed[:, :width].astype(BF),
        summed[:, width : width + top],
        grad_gate[None],
        grad_up[None],
        grad_down[None],
    )


def solution(mesh):
    both = P(("seq", "expert"), None)
    weight = P("expert", "seq", None)
    return jax.shard_map(
        body,
        mesh=mesh,
        in_specs=(both, both, both, both, weight, weight, weight),
        out_specs=(both, both, weight, weight, weight),
        check_vma=False,
    )
```

```python
import jax
import jax.numpy as jnp
from jax import lax
from jax.experimental import pallas as pl
from jax.experimental.pallas import tpu as pltpu
from jax.sharding import PartitionSpec as P

NY, NZ, NC = 4, 8, 2
EARLY = (0, -1, 1, 2)
LATE = (-2, -3, 3, 4)
Y_ORDER = (0, 1, -1, 2)
CAP = 2
PAD = 128
BF = jnp.bfloat16
F32 = jnp.float32
COLS = (((1,), (1,)), ((), ()))
ROWS = (((0,), (0,)), ((), ()))
ANY = pl.BlockSpec(memory_space=pl.ANY)
VMEM = pl.BlockSpec(memory_space=pltpu.VMEM)
SMEM = pl.BlockSpec(memory_space=pltpu.SMEM)


def dot(a, b, dims=(((1,), (0,)), ((), ()))):
    return lax.dot_general(a, b, dims, preferred_element_type=F32)


def tile(n, most):
    return max(b for b in range(PAD, most + 1, PAD) if n % b == 0)


def call(kernel, outs, args, flops, moved, first=(), mib=32, **more):
    specs = dict(
        in_specs=[SMEM if a.dtype == jnp.int32 else VMEM for a in args],
        out_specs=[VMEM] * len(outs),
    )
    specs.update(more)
    specs["in_specs"] = list(specs["in_specs"]) + [ANY] * len(first)
    count = len(args)

    def without(*refs):
        kernel(*refs[:count], *refs[count + len(first) :])

    return pl.pallas_call(
        without,
        out_shape=[jax.ShapeDtypeStruct(s, d) for s, d in outs],
        compiler_params=pltpu.CompilerParams(vmem_limit_bytes=mib * 2**20),
        cost_estimate=pl.CostEstimate(flops=flops, bytes_accessed=moved, transcendentals=0),
        **specs,
    )(*args, *first)


def move(v, dy=0, dz=0, dc=0):
    pairs = []
    for y in range(NY):
        for z in range(NZ):
            for c in range(NC):
                to = (((y + dy) % NY) * NZ + (z + dz) % NZ) * NC + (c + dc) % NC
                pairs.append(((y * NZ + z) * NC + c, to))
    return lax.ppermute(v, "expert", pairs)


def move_x(v, d):
    n = lax.axis_size("seq")
    return lax.ppermute(v, "seq", [(i, (i + d) % n) for i in range(n)])


def lanes(shape):
    return lax.broadcasted_iota(jnp.int32, shape, 1)


def one_hot(slot, slots):
    at = lanes(slot.shape)
    pick = jnp.zeros(slot.shape, F32)
    for d in range(NY):
        of = jnp.sum(jnp.where(at == d, slot, 0.0), axis=1, keepdims=True)
        pick = jnp.where(of == (at - d * slots).astype(F32), 1.0, pick)
    return pick.astype(BF)


def stacked(refs, cols):
    return jnp.concatenate([r[:, cols] for r in refs], axis=0) if len(refs) > 1 else refs[0][:, cols]


def choose(rows, top, width, block, held, groups, slots, into, targets, *refs):
    many = sum(len(group) for group in groups)
    pieces, outs = refs[:many], refs[many:-2]
    slot_out, ids_out = refs[-2:]
    for g, starts in enumerate(groups):
        mine, pieces = pieces[: len(starts)], pieces[len(starts) :]
        mine = [
            p if p.shape[0] <= held else p.at[at : at + held] for p, at in zip(mine, starts)
        ]
        tail = stacked(mine, slice(2 * width, 2 * width + PAD)).astype(F32)
        count = tail.shape[0]
        at = lanes(tail.shape)
        row = lax.broadcasted_iota(jnp.int32, tail.shape, 0)
        ids = jnp.where(at < top, tail, -1.0)
        chosen = jnp.zeros(tail.shape, F32)
        for d in range(NY):
            hit = jnp.where(ids == targets[d].astype(F32), 1.0, 0.0)
            chosen = jnp.where(at == d, jnp.max(hit, axis=1, keepdims=True), chosen)
        r_at = lax.broadcasted_iota(jnp.int32, (count, count), 0)
        c_at = lanes((count, count))
        before = jnp.where((r_at // rows == c_at // rows) & (c_at < r_at), 1.0, 0.0).astype(BF)
        place = dot(before, chosen.astype(BF))
        slot = jnp.where(chosen > 0.0, place + (row // rows * CAP).astype(F32), -4.0 * PAD)
        if g == 0:
            slot_out[...] = slot
            ids_out[...] = ids
        pick = one_hot(slot, slots)
        for j in range(0, 2 * width + PAD, block):
            part = dot(pick, stacked(mine, slice(j, j + block)), ROWS).astype(BF)
            for d in range(NY):
                out, at = into[g][d]
                outs[out][at : at + slots, j : j + block] = part[d * slots : (d + 1) * slots]


def expert(top, block, per_x, sizes, me, *refs):
    *pieces, wg, wu, wd, r_own, r_left, r_right, r_far, hg, dg, du = refs
    pieces = [p.at[:n] for p, n in zip(pieces, sizes)]
    width = wg.shape[1]
    tail = stacked(pieces, slice(2 * width, 2 * width + PAD)).astype(F32)
    gates = pltpu.roll(tail, PAD - top, 1)
    mask = (tail == me[0].astype(F32)) & (lanes(tail.shape) < top)
    gate = jnp.sum(jnp.where(mask, gates, 0.0), axis=1, keepdims=True)
    x = stacked(pieces, slice(0, width))
    pre_gate = dot(x, wg[...], COLS)
    pre_up = dot(x, wu[...], COLS)
    plain = dot(stacked(pieces, slice(width, 2 * width)), wd[...], COLS)
    sig = jax.nn.sigmoid(pre_gate)
    act = pre_gate * sig
    hidden = act * pre_up
    router = jnp.sum(hidden.astype(BF).astype(F32) * plain, axis=1, keepdims=True)
    grad_hidden = gate * plain
    d_gate = (grad_hidden * pre_up * (sig * (1.0 + pre_gate * (1.0 - sig)))).astype(BF)
    d_up = (grad_hidden * act).astype(BF)
    hg[...] = (gate * hidden).astype(BF)
    dg[...] = d_gate
    du[...] = d_up
    outs = (r_own, r_left, r_right, r_far)

    def put(cols, v):
        for out, spans in zip(outs, per_x):
            at = 0
            for start, n in spans:
                out[at : at + n, cols] = v[start : start + n].astype(out.dtype)
                at += n

    for j in range(0, width, block):
        cols = slice(j, j + block)
        put(cols, dot(d_gate, wg[:, cols]) + dot(d_up, wu[:, cols]))
    put(slice(width, width + PAD), jnp.broadcast_to(router, (router.shape[0], PAD)))


def add_up(mine, a, b, c, *outs):
    total = mine[...] + a[...].astype(F32) + b[...].astype(F32) + c[...].astype(F32)
    slots = outs[0].shape[0]
    for d, out in enumerate(outs):
        out[...] = total[d * slots : (d + 1) * slots].astype(BF)


def combine(width, block, targets, slot_e, ids_e, slot_l, ids_l, e0, e1, e2, e3, l0, l1, l2, l3, keep, send):
    slots = l0.shape[0]
    half = keep.shape[0] // 2
    for g, (slot, ids, home) in enumerate(
        ((slot_e, ids_e, (e0, e1, e2, e3)), (slot_l, ids_l, (l0, l1, l2, l3)))
    ):
        pick = one_hot(slot[...], slots)
        narrow = pick[:, : NY * slots]
        rows = slice(g * half, (g + 1) * half)
        for j in range(0, width, block):
            cols = slice(j, j + block)
            part = dot(narrow, stacked(home, cols))
            keep[rows, cols] = part[:half]
            send[rows, cols] = part[half:].astype(BF)
        tail = stacked(home, slice(width, width + PAD))
        at = lanes(narrow.shape)
        routed = jnp.zeros(slot.shape, F32)
        for d in range(NY):
            val = dot(jnp.where(at // slots == d, narrow, jnp.zeros_like(narrow)), tail)
            routed = routed + jnp.where(ids[...] == targets[d].astype(F32), val, 0.0)
        keep[rows, width:] = routed[:half]
        send[rows, width:] = routed[half:].astype(BF)


def outer(many, *refs):
    xs, ys = refs[:many], refs[many : 2 * many]
    *small, o_gate, o_up, o_down = refs[2 * many :]
    third = len(small) // 3
    every = slice(None)
    x, y = stacked(xs, every), stacked(ys, every)
    o_gate[...] = dot(stacked(small[:third], every), x, ROWS).astype(BF)
    o_up[...] = dot(stacked(small[third : 2 * third], every), x, ROWS).astype(BF)
    o_down[...] = dot(stacked(small[2 * third :], every), y, ROWS).astype(BF)


def body(tokens, out_grad, expert_ids, gate_values, gate_weight, up_weight, down_weight):
    rows, width = tokens.shape
    top = expert_ids.shape[1]
    share = gate_weight.shape[1]
    full, back_w = 2 * width + PAD, width + PAD
    me = lax.axis_index("expert").astype(jnp.int32)
    my_y, my_zc = me // (NZ * NC), me % (NZ * NC)
    targets = jnp.stack([((my_y + d) % NY) * (NZ * NC) + my_zc for d in Y_ORDER])
    me = me[None]
    wg, wu, wd = gate_weight[0], up_weight[0], down_weight[0]

    extra = jnp.concatenate(
        [expert_ids.astype(BF), gate_values, jnp.zeros((rows, PAD - 2 * top), BF)], axis=1
    )
    pay = jnp.concatenate([tokens, out_grad, extra], axis=1)

    def both(v):
        return move_x(v, 1), move_x(v, -1)

    def onward(near):
        n = near[0].shape[0] // 2
        return move_x(near[0][:n], 1), move_x(near[1][n:], -1)

    have = {0: pay}
    for d in (1, -1, 2, -2):
        have[d] = move(pay, dz=-d)
    early = jnp.concatenate([have[d] for d in EARLY], axis=0)
    early_near = both(early)
    far_z = [move(have[-2][:, :width], dz=2), move(have[2][:, width:], dz=-2)]
    have[-3], have[3] = move(have[-2], dz=1), move(have[2], dz=-1)
    have[NZ // 2] = jnp.concatenate(far_z, axis=1)
    late = jnp.concatenate([have[d] for d in LATE], axis=0)
    held = rows * len(EARLY)
    count = NC * held
    slots = count // rows * CAP

    def choosing(groups, into, outs, pieces, first=()):
        def kernel(*refs):
            choose(rows, top, width, tile(full, 1664), held, groups, slots, into, *refs)

        return call(
            kernel,
            [((n, full), BF) for n in outs] + [((count, PAD), F32)] * 2,
            (targets, *pieces),
            2 * count * PAD * full * len(groups),
            4 * count * full * len(groups),
            first,
        )

    late_other, early_other = move(late, dc=1), move(early, dc=1)
    l0, l1, l2, l3, slot_l, ids_l = choosing(
        [[0, 0]], [[(d, 0) for d in range(NY)]], [slots] * NY, (late, late_other), (early_other,)
    )

    l1, l2 = move(l1, dy=1), move(l2, dy=-1)

    def cut(left, right, top_half, low_half, two):
        n, half = left.shape[0], top_half.shape[0]
        top_half[...] = left[:half]
        low_half[...] = right[half:]
        two[:n] = left[...]
        two[n:] = right[...]

    top_half, low_half, two = call(
        cut,
        [((held // 2, full), BF)] * 2 + [((2 * held, full), BF)],
        early_near,
        0,
        8 * held * full,
        (l1, l2),
    )
    early_far = move_x(top_half, 1), move_x(low_half, -1)
    two_other = move(two, dc=1)
    far_other = [move(p, dc=1) for p in early_far]

    def join(*refs):
        *ins, out = refs
        for i, piece in enumerate(ins):
            out[i * slots : (i + 1) * slots] = piece[...]

    (late,) = call(
        join,
        [((NY * slots, full), BF)],
        (l0, l1, l2, move(l3, dy=2)),
        0,
        16 * slots * full,
        far_other,
    )
    late_near = both(late)
    all_x, part_x = 4 * slots, 2 * slots
    into = [
        [(0, x * slots), (1, x * slots), (2, x * slots), (1 + x // 2, all_x + x % 2 * slots)]
        for x in range(4)
    ]
    groups = (
        [(early, 0), (early_other, 0)],
        [(two, 0), (two_other, 0)],
        [(two, held), (two_other, held)],
        [(p, 0) for p in (*early_far, *far_other)],
    )
    pieces = [p for group in groups for p, _ in group]
    starts = [[at for _, at in group] for group in groups]
    e0, e1, e2, slot_e, ids_e = choosing(
        starts, into, [all_x, all_x + part_x, all_x + part_x], pieces
    )
    e1, e2 = move(e1, dy=1), move(e2, dy=-1)
    early_parts = [e0, e1, e2, move(e1[all_x:], dy=1), move(e2[all_x:], dy=-1)]
    early_sizes = [all_x] * 3 + [part_x] * 2
    late_far = onward(late_near)

    def back_and_forth(parts, sizes, per_x, first=()):
        def kernel(*refs):
            expert(top, tile(width, 1024), per_x, sizes, *refs)

        n = sum(sizes)
        r_own, r_left, r_right, r_far, hg, dg, du = call(
            kernel,
            [((n // 4, back_w), F32)] + [((n // 4, back_w), BF)] * 3 + [((n, share), BF)] * 3,
            (me, *parts, wg, wu, wd),
            2 * n * width * share * 5,
            2 * (n * full + n * back_w + 3 * share * width),
            first,
        )
        return (dg, du, hg), r_own, (move_x(r_far, 2), move_x(r_left, -1), move_x(r_right, 1))

    def spans(many, n):
        return [[(i * 4 * n + x * n, n) for i in range(many)] for x in range(4)]

    late_parts = [late, *late_near, *late_far]
    late_sizes = [p.shape[0] for p in late_parts]
    small_l, own_l, got_l = back_and_forth(late_parts, late_sizes, spans(1, NY * slots))
    small_e, own_e, got_e = back_and_forth(early_parts, early_sizes, spans(NY, slots), (own_l,))

    block = tile(width, 512)
    steps = width // block
    parts = [*late_parts, *early_parts]
    sizes = late_sizes + early_sizes
    small = [a for group in zip(small_l, small_e) for a in group]

    def outer_k(*refs):
        outer(len(parts), *refs)

    grad_gate, grad_up, grad_down = call(
        outer_k,
        [((share, width), BF)] * 3,
        parts + parts + small,
        2 * 3 * 8 * count * share * width,
        2 * (8 * count * full + 3 * share * width),
        got_l,
        grid=(steps,),
        in_specs=[pl.BlockSpec((n, block), lambda j: (0, j)) for n in sizes]
        + [pl.BlockSpec((n, block), lambda j: (0, j + steps)) for n in sizes]
        + [pl.BlockSpec(a.shape, lambda j: (0, 0)) for a in small],
        out_specs=[pl.BlockSpec((share, block), lambda j: (0, j))] * 3,
    )

    def home(own, got, first):
        h0, h1, h2, h3 = call(
            add_up,
            [((slots, back_w), BF)] * NY,
            (own, *got),
            0,
            20 * count * back_w,
            first,
        )
        return h0, move(h1, dy=-1), move(h2, dy=1), move(h3, dy=2)

    home_l = home(own_l, got_l, ())
    home_e = home(own_e, got_e, (grad_down,))

    def combine_k(*refs):
        combine(width, tile(width, 1024), *refs)

    keep, send = call(
        combine_k,
        [((count, back_w), F32), ((count, back_w), BF)],
        (targets, slot_e, ids_e, slot_l, ids_l, *home_e, *home_l),
        4 * count * count * back_w,
        10 * count * back_w,
    )
    cored = keep + move(send, dc=1).astype(F32)
    sent = cored.astype(BF)
    summed = cored[:rows]
    for b, d in enumerate(EARLY + LATE):
        if d:
            summed = summed + move(sent[b * rows : (b + 1) * rows], dz=d).astype(F32)
    return (
        summed[:, :width].astype(BF),
        summed[:, width : width + top],
        grad_gate[None],
        grad_up[None],
        grad_down[None],
    )


def solution(mesh):
    both = P(("seq", "expert"), None)
    weight = P("expert", "seq", None)
    return jax.shard_map(
        body,
        mesh=mesh,
        in_specs=(both, both, both, both, weight, weight, weight),
        out_specs=(both, both, weight, weight, weight),
        check_vma=False,
    )
```

```python
import jax
import jax.numpy as jnp
from jax import lax
from jax.experimental import pallas as pl
from jax.experimental.pallas import tpu as pltpu
from jax.sharding import PartitionSpec as P

NY, NZ, NC = 4, 8, 2
Y_ORDER = (0, 1, -1, 2)
CAP = 2
PAD = 128
BF = jnp.bfloat16
F32 = jnp.float32
COLS = (((1,), (1,)), ((), ()))
ROWS = (((0,), (0,)), ((), ()))
ANY = pl.BlockSpec(memory_space=pl.ANY)
VMEM = pl.BlockSpec(memory_space=pltpu.VMEM)
SMEM = pl.BlockSpec(memory_space=pltpu.SMEM)


def dot(a, b, dims=(((1,), (0,)), ((), ()))):
    return lax.dot_general(a, b, dims, preferred_element_type=F32)


def tile(n, most):
    return max(b for b in range(PAD, most + 1, PAD) if n % b == 0)


def call(kernel, outs, args, flops, moved, first=(), mib=32, **more):
    specs = dict(
        in_specs=[SMEM if a.dtype == jnp.int32 else VMEM for a in args],
        out_specs=[VMEM] * len(outs),
    )
    specs.update(more)
    specs["in_specs"] = list(specs["in_specs"]) + [ANY] * len(first)
    count = len(args)

    def without(*refs):
        kernel(*refs[:count], *refs[count + len(first) :])

    return pl.pallas_call(
        without,
        out_shape=[jax.ShapeDtypeStruct(s, d) for s, d in outs],
        compiler_params=pltpu.CompilerParams(vmem_limit_bytes=mib * 2**20),
        cost_estimate=pl.CostEstimate(flops=flops, bytes_accessed=moved, transcendentals=0),
        **specs,
    )(*args, *first)


def move(v, dy=0, dz=0, dc=0):
    pairs = []
    for y in range(NY):
        for z in range(NZ):
            for c in range(NC):
                to = (((y + dy) % NY) * NZ + (z + dz) % NZ) * NC + (c + dc) % NC
                pairs.append(((y * NZ + z) * NC + c, to))
    return lax.ppermute(v, "expert", pairs)


def move_x(v, d):
    n = lax.axis_size("seq")
    return lax.ppermute(v, "seq", [(i, (i + d) % n) for i in range(n)])


def move_split(v, dx=0, dz=0):
    n = lax.axis_size("seq")
    pairs = []
    for x in range(n):
        for e in range(NY * NZ * NC):
            y, z, c = e // (NZ * NC), e // NC % NZ, e % NC
            sign = 1 - 2 * c
            to = (y * NZ + (z + sign * dz) % NZ) * NC + c
            pairs.append((x * NY * NZ * NC + e, (x + sign * dx) % n * NY * NZ * NC + to))
    return lax.ppermute(v, ("seq", "expert"), pairs)


def lanes(shape):
    return lax.broadcasted_iota(jnp.int32, shape, 1)


def one_hot(slot, slots):
    at = lanes(slot.shape)
    pick = jnp.zeros(slot.shape, F32)
    for d in range(NY):
        of = jnp.sum(jnp.where(at == d, slot, 0.0), axis=1, keepdims=True)
        pick = jnp.where(of == (at - d * slots).astype(F32), 1.0, pick)
    return pick.astype(BF)


def stacked(refs, cols):
    return jnp.concatenate([r[:, cols] for r in refs], axis=0) if len(refs) > 1 else refs[0][:, cols]


def choose(rows, top, width, block, groups, slots, into, targets, *refs):
    many = sum(groups)
    pieces, outs = refs[:many], refs[many:-2]
    slot_out, ids_out = refs[-2:]
    for g, n in enumerate(groups):
        mine, pieces = pieces[:n], pieces[n:]
        tail = stacked(mine, slice(2 * width, 2 * width + PAD)).astype(F32)
        count = tail.shape[0]
        at = lanes(tail.shape)
        row = lax.broadcasted_iota(jnp.int32, tail.shape, 0)
        ids = jnp.where(at < top, tail, -1.0)
        chosen = jnp.zeros(tail.shape, F32)
        for d in range(NY):
            hit = jnp.where(ids == targets[d].astype(F32), 1.0, 0.0)
            chosen = jnp.where(at == d, jnp.max(hit, axis=1, keepdims=True), chosen)
        r_at = lax.broadcasted_iota(jnp.int32, (count, count), 0)
        c_at = lanes((count, count))
        before = jnp.where((r_at // rows == c_at // rows) & (c_at < r_at), 1.0, 0.0).astype(BF)
        place = dot(before, chosen.astype(BF))
        first = row // rows * CAP
        if n == 2:
            first = (first + targets[NY] * (slots // 2)) % slots
        slot = jnp.where(chosen > 0.0, place + first.astype(F32), -4.0 * PAD)
        if g == 0:
            slot_out[...] = slot
            ids_out[...] = ids
        pick = one_hot(slot, slots)
        for j in range(0, 2 * width + PAD, block):
            part = dot(pick, stacked(mine, slice(j, j + block)), ROWS).astype(BF)
            for d in range(NY):
                out, at = into[g][d]
                outs[out][at : at + slots, j : j + block] = part[d * slots : (d + 1) * slots]


def expert(top, block, per_x, sizes, me, *refs):
    *pieces, wg, wu, wd, r_own, r_left, r_right, r_far, hg, dg, du = refs
    pieces = [p.at[:n] for p, n in zip(pieces, sizes)]
    width = wg.shape[1]
    tail = stacked(pieces, slice(2 * width, 2 * width + PAD)).astype(F32)
    gates = pltpu.roll(tail, PAD - top, 1)
    mask = (tail == me[0].astype(F32)) & (lanes(tail.shape) < top)
    gate = jnp.sum(jnp.where(mask, gates, 0.0), axis=1, keepdims=True)
    x = stacked(pieces, slice(0, width))
    pre_gate = dot(x, wg[...], COLS)
    pre_up = dot(x, wu[...], COLS)
    plain = dot(stacked(pieces, slice(width, 2 * width)), wd[...], COLS)
    sig = jax.nn.sigmoid(pre_gate)
    act = pre_gate * sig
    hidden = act * pre_up
    router = jnp.sum(hidden.astype(BF).astype(F32) * plain, axis=1, keepdims=True)
    grad_hidden = gate * plain
    d_gate = (grad_hidden * pre_up * (sig * (1.0 + pre_gate * (1.0 - sig)))).astype(BF)
    d_up = (grad_hidden * act).astype(BF)
    hg[...] = (gate * hidden).astype(BF)
    dg[...] = d_gate
    du[...] = d_up
    outs = (r_own, r_left, r_right, r_far)

    def put(cols, v):
        for out, spans in zip(outs, per_x):
            at = 0
            for start, n in spans:
                out[at : at + n, cols] = v[start : start + n].astype(out.dtype)
                at += n

    for j in range(0, width, block):
        cols = slice(j, j + block)
        put(cols, dot(d_gate, wg[:, cols]) + dot(d_up, wu[:, cols]))
    put(slice(width, width + PAD), jnp.broadcast_to(router, (router.shape[0], PAD)))


def add_up(mine, a, b, c, *outs):
    total = mine[...] + a[...].astype(F32) + b[...].astype(F32) + c[...].astype(F32)
    slots = outs[0].shape[0]
    for d, out in enumerate(outs):
        out[...] = total[d * slots : (d + 1) * slots].astype(BF)


def combine(width, block, targets, slot_e, ids_e, slot_l, ids_l, e0, e1, e2, e3, l0, l1, l2, l3, keep, send):
    slots = l0.shape[0]
    n = keep.shape[0] // 4
    first = targets[NY] == 0
    narrow = [one_hot(slot[...], slots)[:, : NY * slots] for slot in (slot_e, slot_l)]
    homes = ((e0, e1, e2, e3), (l0, l1, l2, l3))

    def give(cols, e, l):
        e0, em1, ep1, em2 = (e[i * n : (i + 1) * n] for i in range(4))
        lp2, lm3, lp3, l4 = (l[i * n : (i + 1) * n] for i in range(4))
        plus = jnp.concatenate([ep1, lp2, lp3, e0[: n // 2], l4[: n // 2]], axis=0)
        minus = jnp.concatenate([em1, em2, lm3, e0[n // 2 :], l4[n // 2 :]], axis=0)
        keep[:, cols] = jnp.where(first, plus, minus)
        send[:, cols] = jnp.where(first, minus, plus).astype(BF)

    for j in range(0, width, block):
        cols = slice(j, j + block)
        give(cols, *(dot(p, stacked(home, cols)) for p, home in zip(narrow, homes)))
    tails = []
    for p, home, ids in zip(narrow, homes, (ids_e, ids_l)):
        tail = stacked(home, slice(width, width + PAD))
        at = lanes(p.shape)
        routed = jnp.zeros(ids.shape, F32)
        for d in range(NY):
            val = dot(jnp.where(at // slots == d, p, jnp.zeros_like(p)), tail)
            routed = routed + jnp.where(ids[...] == targets[d].astype(F32), val, 0.0)
        tails.append(routed)
    give(slice(width, width + PAD), *tails)


def outer(many, *refs):
    xs, ys = refs[:many], refs[many : 2 * many]
    *small, o_gate, o_up, o_down = refs[2 * many :]
    third = len(small) // 3
    every = slice(None)
    x, y = stacked(xs, every), stacked(ys, every)
    o_gate[...] = dot(stacked(small[:third], every), x, ROWS).astype(BF)
    o_up[...] = dot(stacked(small[third : 2 * third], every), x, ROWS).astype(BF)
    o_down[...] = dot(stacked(small[2 * third :], every), y, ROWS).astype(BF)


def body(tokens, out_grad, expert_ids, gate_values, gate_weight, up_weight, down_weight):
    rows, width = tokens.shape
    top = expert_ids.shape[1]
    share = gate_weight.shape[1]
    full, back_w = 2 * width + PAD, width + PAD
    me = lax.axis_index("expert").astype(jnp.int32)
    my_y, my_zc = me // (NZ * NC), me % (NZ * NC)
    core = me % NC
    targets = jnp.stack([((my_y + d) % NY) * (NZ * NC) + my_zc for d in Y_ORDER] + [core])
    me = me[None]
    wg, wu, wd = gate_weight[0], up_weight[0], down_weight[0]

    extra = jnp.concatenate(
        [expert_ids.astype(BF), gate_values, jnp.zeros((rows, PAD - 2 * top), BF)], axis=1
    )
    pay = jnp.concatenate([tokens, out_grad, extra], axis=1)

    def both(v):
        return move_x(v, 1), move_x(v, -1)

    def onward(near):
        n = near[0].shape[0] // 2
        return move_x(near[0][:n], 1), move_x(near[1][n:], -1)

    across = move(pay, dc=1)
    pair = jnp.concatenate(
        [jnp.where(core == 0, pay, across), jnp.where(core == 0, across, pay)], axis=0
    )
    one, two = move_split(pair, dz=1), move_split(pair, dz=2)
    three = move_split(two, dz=1)
    four = move_split(lax.dynamic_slice_in_dim(two, core * width, width + PAD, 1), dz=2)
    one_o, two_o, three_o, four_o = (move(v, dc=1) for v in (one, two, three, four))
    n = NC * rows
    held = 4 * n
    count = held
    slots = count // rows * CAP

    def early_k(targets, pair, one, one_o, two, two_o, out):
        out[:n] = pair[...]

        def fill(minus, plus, last):
            out[n : 2 * n] = minus[...]
            out[2 * n : 3 * n] = plus[...]
            out[3 * n :] = last[...]

        pl.when(targets[NY] == 0)(lambda: fill(one, one_o, two))
        pl.when(targets[NY] == 1)(lambda: fill(one_o, one, two_o))

    def late_k(targets, two, two_o, three, three_o, four, four_o, out):
        def fill(plus2, minus3, plus3, low, high):
            out[:n] = plus2[...]
            out[n : 2 * n] = minus3[...]
            out[2 * n : 3 * n] = plus3[...]
            out[3 * n :, : width + PAD] = low[...]
            out[3 * n :, width:] = high[...]

        pl.when(targets[NY] == 0)(lambda: fill(two_o, three, three_o, four, four_o))
        pl.when(targets[NY] == 1)(lambda: fill(two, three_o, three, four_o, four))

    moved = 4 * held * full
    (early,) = call(
        early_k, [((held, full), BF)], (targets, pair, one, one_o, two, two_o), 0, moved
    )
    near = move_split(early, dx=1)
    (late,) = call(
        late_k,
        [((held, full), BF)],
        (targets, two, two_o, three, three_o, four, four_o),
        0,
        moved,
    )

    def choosing(groups, into, outs, pieces, first=()):
        def kernel(*refs):
            choose(rows, top, width, tile(full, 1664), groups, slots, into, *refs)

        return call(
            kernel,
            [((n, full), BF) for n in outs] + [((count, PAD), F32)] * 2,
            (targets, *pieces),
            2 * count * PAD * full * len(groups),
            4 * count * full * len(groups),
            first,
        )

    l0, l1, l2, l3, slot_l, ids_l = choosing(
        (1,), [[(d, 0) for d in range(NY)]], [slots] * NY, (late,)
    )
    l1, l2 = move(l1, dy=1), move(l2, dy=-1)

    def cut(targets, near, half, whole):
        m = half.shape[0]
        whole[...] = near[...]

        def fill(at):
            half[...] = near[at : at + m]

        pl.when(targets[NY] == 0)(lambda: fill(0))
        pl.when(targets[NY] == 1)(lambda: fill(m))

    half, near = call(
        cut,
        [((held // 2, full), BF), ((held, full), BF)],
        (targets, near),
        0,
        moved,
        (l1, l2),
    )
    far = move_split(half, dx=1)
    near_o, far_o = move(near, dc=1), move(far, dc=1)

    def join(*refs):
        *ins, out = refs
        for i, piece in enumerate(ins):
            out[i * slots : (i + 1) * slots] = piece[...]

    (late,) = call(
        join,
        [((NY * slots, full), BF)],
        (l0, l1, l2, move(l3, dy=2)),
        0,
        16 * slots * full,
        (far_o,),
    )
    late_near = both(late)
    all_x, part_x = 4 * slots, 2 * slots
    into = [
        [(0, x * slots), (1, x * slots), (2, x * slots), (1 + x // 2, all_x + x % 2 * slots)]
        for x in range(4)
    ]
    e0, e1, e2, slot_e, ids_e = choosing(
        (1, 1, 1, 2),
        into,
        [all_x, all_x + part_x, all_x + part_x],
        (early, near, near_o, far, far_o),
    )
    e1, e2 = move(e1, dy=1), move(e2, dy=-1)
    early_parts = [e0, e1, e2, move(e1[all_x:], dy=1), move(e2[all_x:], dy=-1)]
    early_sizes = [all_x] * 3 + [part_x] * 2
    late_far = onward(late_near)

    def back_and_forth(parts, sizes, per_x, first=()):
        def kernel(*refs):
            expert(top, tile(width, 1024), per_x, sizes, *refs)

        n = sum(sizes)
        r_own, r_left, r_right, r_far, hg, dg, du = call(
            kernel,
            [((n // 4, back_w), F32)] + [((n // 4, back_w), BF)] * 3 + [((n, share), BF)] * 3,
            (me, *parts, wg, wu, wd),
            2 * n * width * share * 5,
            2 * (n * full + n * back_w + 3 * share * width),
            first,
        )
        return (dg, du, hg), r_own, (r_left, r_right, r_far)

    def spans(many, n):
        return [[(i * 4 * n + x * n, n) for i in range(many)] for x in range(4)]

    late_parts = [late, *late_near, *late_far]
    late_sizes = [p.shape[0] for p in late_parts]
    small_l, own_l, sums = back_and_forth(late_parts, late_sizes, spans(1, NY * slots))
    got_l = move_x(sums[2], 2), move_x(sums[0], -1), move_x(sums[1], 1)
    small_e, own_e, sums = back_and_forth(early_parts, early_sizes, spans(NY, slots), (own_l,))
    got_e = move_x(sums[2], 2), move_split(sums[0], dx=-1), move_split(sums[1], dx=1)

    block = tile(width, 512)
    steps = width // block
    parts = [*late_parts, *early_parts]
    sizes = late_sizes + early_sizes
    small = [a for group in zip(small_l, small_e) for a in group]

    def outer_k(*refs):
        outer(len(parts), *refs)

    grad_gate, grad_up, grad_down = call(
        outer_k,
        [((share, width), BF)] * 3,
        parts + parts + small,
        2 * 3 * 8 * count * share * width,
        2 * (8 * count * full + 3 * share * width),
        got_l,
        grid=(steps,),
        in_specs=[pl.BlockSpec((n, block), lambda j: (0, j)) for n in sizes]
        + [pl.BlockSpec((n, block), lambda j: (0, j + steps)) for n in sizes]
        + [pl.BlockSpec(a.shape, lambda j: (0, 0)) for a in small],
        out_specs=[pl.BlockSpec((share, block), lambda j: (0, j))] * 3,
    )

    def home(own, got, first):
        h0, h1, h2, h3 = call(
            add_up,
            [((slots, back_w), BF)] * NY,
            (own, *got),
            0,
            20 * count * back_w,
            first,
        )
        return h0, move(h1, dy=-1), move(h2, dy=1), move(h3, dy=2)

    home_l = home(own_l, got_l, ())
    home_e = home(own_e, got_e, (grad_down,))

    def combine_k(*refs):
        combine(width, tile(width, 1024), *refs)

    keep, send = call(
        combine_k,
        [((count, back_w), F32), ((count, back_w), BF)],
        (targets, slot_e, ids_e, slot_l, ids_l, *home_e, *home_l),
        4 * count * count * back_w,
        10 * count * back_w,
    )
    cored = keep + move(send, dc=1).astype(F32)
    sent = cored.astype(BF)
    apart = sum(move_split(sent[i * n : (i + 1) * n], dz=i + 1).astype(F32) for i in range(3))
    opposite = move_split(sent[3 * n + rows :], dz=NZ // 2).astype(F32)
    ours = jnp.where(core == 0, apart[:rows], apart[rows:])
    theirs = jnp.where(core == 0, apart[rows:], apart[:rows])
    summed = cored[3 * n : 3 * n + rows] + opposite + ours
    summed = summed + move(theirs.astype(BF), dc=1).astype(F32)
    return (
        summed[:, :width].astype(BF),
        summed[:, width : width + top],
        grad_gate[None],
        grad_up[None],
        grad_down[None],
    )


def solution(mesh):
    both = P(("seq", "expert"), None)
    weight = P("expert", "seq", None)
    return jax.shard_map(
        body,
        mesh=mesh,
        in_specs=(both, both, both, both, weight, weight, weight),
        out_specs=(both, both, weight, weight, weight),
        check_vma=False,
    )
```

```python
import jax
import jax.numpy as jnp
from jax import lax
from jax.experimental import pallas as pl
from jax.experimental.pallas import tpu as pltpu
from jax.sharding import PartitionSpec as P

NY, NZ, NC = 4, 8, 2
Y_ORDER = (0, 1, -1, 2)
CAP = 2
PAD = 128
BF = jnp.bfloat16
F32 = jnp.float32
COLS = (((1,), (1,)), ((), ()))
ROWS = (((0,), (0,)), ((), ()))
ANY = pl.BlockSpec(memory_space=pl.ANY)
VMEM = pl.BlockSpec(memory_space=pltpu.VMEM)
SMEM = pl.BlockSpec(memory_space=pltpu.SMEM)


def dot(a, b, dims=(((1,), (0,)), ((), ()))):
    return lax.dot_general(a, b, dims, preferred_element_type=F32)


def tile(n, most):
    return max(b for b in range(PAD, most + 1, PAD) if n % b == 0)


def call(kernel, outs, args, flops, moved, first=(), mib=32, **more):
    specs = dict(
        in_specs=[SMEM if a.dtype == jnp.int32 else VMEM for a in args],
        out_specs=[VMEM] * len(outs),
    )
    specs.update(more)
    specs["in_specs"] = list(specs["in_specs"]) + [ANY] * len(first)
    count = len(args)

    def without(*refs):
        kernel(*refs[:count], *refs[count + len(first) :])

    return pl.pallas_call(
        without,
        out_shape=[jax.ShapeDtypeStruct(s, d) for s, d in outs],
        compiler_params=pltpu.CompilerParams(vmem_limit_bytes=mib * 2**20),
        cost_estimate=pl.CostEstimate(flops=flops, bytes_accessed=moved, transcendentals=0),
        **specs,
    )(*args, *first)


def move(v, dy=0, dz=0, dc=0):
    pairs = []
    for y in range(NY):
        for z in range(NZ):
            for c in range(NC):
                to = (((y + dy) % NY) * NZ + (z + dz) % NZ) * NC + (c + dc) % NC
                pairs.append(((y * NZ + z) * NC + c, to))
    return lax.ppermute(v, "expert", pairs)


def move_x(v, d):
    n = lax.axis_size("seq")
    return lax.ppermute(v, "seq", [(i, (i + d) % n) for i in range(n)])


def move_split(v, dx=0, dz=0):
    n = lax.axis_size("seq")
    pairs = []
    for x in range(n):
        for e in range(NY * NZ * NC):
            y, z, c = e // (NZ * NC), e // NC % NZ, e % NC
            sign = 1 - 2 * c
            to = (y * NZ + (z + sign * dz) % NZ) * NC + c
            pairs.append((x * NY * NZ * NC + e, (x + sign * dx) % n * NY * NZ * NC + to))
    return lax.ppermute(v, ("seq", "expert"), pairs)


def lanes(shape):
    return lax.broadcasted_iota(jnp.int32, shape, 1)


def one_hot(slot, slots):
    at = lanes(slot.shape)
    pick = jnp.zeros(slot.shape, F32)
    for d in range(NY):
        of = jnp.sum(jnp.where(at == d, slot, 0.0), axis=1, keepdims=True)
        pick = jnp.where(of == (at - d * slots).astype(F32), 1.0, pick)
    return pick.astype(BF)


def stacked(refs, cols):
    return jnp.concatenate([r[:, cols] for r in refs], axis=0) if len(refs) > 1 else refs[0][:, cols]


def choose(rows, top, width, block, groups, slots, into, targets, *refs):
    many = sum(groups)
    pieces, outs = refs[:many], refs[many:-2]
    slot_out, ids_out = refs[-2:]
    for g, n in enumerate(groups):
        mine, pieces = pieces[:n], pieces[n:]
        tail = stacked(mine, slice(2 * width, 2 * width + PAD)).astype(F32)
        count = tail.shape[0]
        at = lanes(tail.shape)
        row = lax.broadcasted_iota(jnp.int32, tail.shape, 0)
        ids = jnp.where(at < top, tail, -1.0)
        chosen = jnp.zeros(tail.shape, F32)
        for d in range(NY):
            hit = jnp.where(ids == targets[d].astype(F32), 1.0, 0.0)
            chosen = jnp.where(at == d, jnp.max(hit, axis=1, keepdims=True), chosen)
        r_at = lax.broadcasted_iota(jnp.int32, (count, count), 0)
        c_at = lanes((count, count))
        before = jnp.where((r_at // rows == c_at // rows) & (c_at < r_at), 1.0, 0.0).astype(BF)
        place = dot(before, chosen.astype(BF))
        first = row // rows * CAP
        if n == 2:
            first = (first + targets[NY] * (slots // 2)) % slots
        slot = jnp.where(chosen > 0.0, place + first.astype(F32), -4.0 * PAD)
        if g == 0:
            slot_out[...] = slot
            ids_out[...] = ids
        pick = one_hot(slot, slots)
        for j in range(0, 2 * width + PAD, block):
            part = dot(pick, stacked(mine, slice(j, j + block)), ROWS).astype(BF)
            for d in range(NY):
                out, at = into[g][d]
                outs[out][at : at + slots, j : j + block] = part[d * slots : (d + 1) * slots]


def expert(top, block, per_x, sizes, me, *refs):
    *pieces, wg, wu, wd, r_own, r_left, r_right, r_fa, r_fb, hg, dg, du = refs
    pieces = [p.at[:n] for p, n in zip(pieces, sizes)]
    width = wg.shape[1]
    tail = stacked(pieces, slice(2 * width, 2 * width + PAD)).astype(F32)
    gates = pltpu.roll(tail, PAD - top, 1)
    mask = (tail == me[0].astype(F32)) & (lanes(tail.shape) < top)
    gate = jnp.sum(jnp.where(mask, gates, 0.0), axis=1, keepdims=True)
    x = stacked(pieces, slice(0, width))
    pre_gate = dot(x, wg[...], COLS)
    pre_up = dot(x, wu[...], COLS)
    plain = dot(stacked(pieces, slice(width, 2 * width)), wd[...], COLS)
    sig = jax.nn.sigmoid(pre_gate)
    act = pre_gate * sig
    hidden = act * pre_up
    router = jnp.sum(hidden.astype(BF).astype(F32) * plain, axis=1, keepdims=True)
    grad_hidden = gate * plain
    d_gate = (grad_hidden * pre_up * (sig * (1.0 + pre_gate * (1.0 - sig)))).astype(BF)
    d_up = (grad_hidden * act).astype(BF)
    hg[...] = (gate * hidden).astype(BF)
    dg[...] = d_gate
    du[...] = d_up
    outs = (r_own, r_left, r_right, r_fa, r_fb)

    def put(cols, v):
        for out, spans in zip(outs, per_x):
            at = 0
            for start, n in spans:
                out[at : at + n, cols] = v[start : start + n].astype(out.dtype)
                at += n

    for j in range(0, width, block):
        cols = slice(j, j + block)
        put(cols, dot(d_gate, wg[:, cols]) + dot(d_up, wu[:, cols]))
    put(slice(width, width + PAD), jnp.broadcast_to(router, (router.shape[0], PAD)))


def pass_on(left, right, via_left, via_right, to_left, to_right):
    m = via_left.shape[0]
    to_left[:m] = left[:m]
    to_left[m:] = (left[m:].astype(F32) + via_right[...].astype(F32)).astype(BF)
    to_right[:m] = (right[:m].astype(F32) + via_left[...].astype(F32)).astype(BF)
    to_right[m:] = right[m:]


def add_up(mine, a, b, *outs):
    total = mine[...] + a[...].astype(F32) + b[...].astype(F32)
    slots = outs[0].shape[0]
    for d, out in enumerate(outs):
        out[...] = total[d * slots : (d + 1) * slots].astype(BF)


def combine(width, block, targets, slot_e, ids_e, slot_l, ids_l, e0, e1, e2, e3, l0, l1, l2, l3, keep, send):
    slots = l0.shape[0]
    n = keep.shape[0] // 4
    first = targets[NY] == 0
    narrow = [one_hot(slot[...], slots)[:, : NY * slots] for slot in (slot_e, slot_l)]
    homes = ((e0, e1, e2, e3), (l0, l1, l2, l3))

    def give(cols, e, l):
        e0, em1, ep1, em2 = (e[i * n : (i + 1) * n] for i in range(4))
        lp2, lm3, lp3, l4 = (l[i * n : (i + 1) * n] for i in range(4))
        plus = jnp.concatenate([ep1, lp2, lp3, e0[: n // 2], l4[: n // 2]], axis=0)
        minus = jnp.concatenate([em1, em2, lm3, e0[n // 2 :], l4[n // 2 :]], axis=0)
        keep[:, cols] = jnp.where(first, plus, minus)
        send[:, cols] = jnp.where(first, minus, plus).astype(BF)

    for j in range(0, width, block):
        cols = slice(j, j + block)
        give(cols, *(dot(p, stacked(home, cols)) for p, home in zip(narrow, homes)))
    tails = []
    for p, home, ids in zip(narrow, homes, (ids_e, ids_l)):
        tail = stacked(home, slice(width, width + PAD))
        at = lanes(p.shape)
        routed = jnp.zeros(ids.shape, F32)
        for d in range(NY):
            val = dot(jnp.where(at // slots == d, p, jnp.zeros_like(p)), tail)
            routed = routed + jnp.where(ids[...] == targets[d].astype(F32), val, 0.0)
        tails.append(routed)
    give(slice(width, width + PAD), *tails)


def outer(many, *refs):
    xs, ys = refs[:many], refs[many : 2 * many]
    *small, o_gate, o_up, o_down = refs[2 * many :]
    third = len(small) // 3
    every = slice(None)
    x, y = stacked(xs, every), stacked(ys, every)
    o_gate[...] = dot(stacked(small[:third], every), x, ROWS).astype(BF)
    o_up[...] = dot(stacked(small[third : 2 * third], every), x, ROWS).astype(BF)
    o_down[...] = dot(stacked(small[2 * third :], every), y, ROWS).astype(BF)


def body(tokens, out_grad, expert_ids, gate_values, gate_weight, up_weight, down_weight):
    rows, width = tokens.shape
    top = expert_ids.shape[1]
    share = gate_weight.shape[1]
    full, back_w = 2 * width + PAD, width + PAD
    me = lax.axis_index("expert").astype(jnp.int32)
    my_y, my_zc = me // (NZ * NC), me % (NZ * NC)
    core = me % NC
    targets = jnp.stack([((my_y + d) % NY) * (NZ * NC) + my_zc for d in Y_ORDER] + [core])
    me = me[None]
    wg, wu, wd = gate_weight[0], up_weight[0], down_weight[0]

    extra = jnp.concatenate(
        [expert_ids.astype(BF), gate_values, jnp.zeros((rows, PAD - 2 * top), BF)], axis=1
    )
    pay = jnp.concatenate([tokens, out_grad, extra], axis=1)

    def both(v):
        return move_x(v, 1), move_x(v, -1)

    def onward(near):
        n = near[0].shape[0] // 2
        return move_x(near[0][:n], 1), move_x(near[1][n:], -1)

    across = move(pay, dc=1)
    pair = jnp.concatenate(
        [jnp.where(core == 0, pay, across), jnp.where(core == 0, across, pay)], axis=0
    )
    one, two = move_split(pair, dz=1), move_split(pair, dz=2)
    three = move_split(two, dz=1)
    four = move_split(lax.dynamic_slice_in_dim(two, core * width, width + PAD, 1), dz=2)
    one_o, two_o, three_o, four_o = (move(v, dc=1) for v in (one, two, three, four))
    n = NC * rows
    held = 4 * n
    count = held
    slots = count // rows * CAP

    def early_k(targets, pair, one, one_o, two, two_o, out):
        out[:n] = pair[...]

        def fill(minus, plus, last):
            out[n : 2 * n] = minus[...]
            out[2 * n : 3 * n] = plus[...]
            out[3 * n :] = last[...]

        pl.when(targets[NY] == 0)(lambda: fill(one, one_o, two))
        pl.when(targets[NY] == 1)(lambda: fill(one_o, one, two_o))

    def late_k(targets, two, two_o, three, three_o, four, four_o, out):
        def fill(plus2, minus3, plus3, low, high):
            out[:n] = plus2[...]
            out[n : 2 * n] = minus3[...]
            out[2 * n : 3 * n] = plus3[...]
            out[3 * n :, : width + PAD] = low[...]
            out[3 * n :, width:] = high[...]

        pl.when(targets[NY] == 0)(lambda: fill(two_o, three, three_o, four, four_o))
        pl.when(targets[NY] == 1)(lambda: fill(two, three_o, three, four_o, four))

    moved = 4 * held * full
    (early,) = call(
        early_k, [((held, full), BF)], (targets, pair, one, one_o, two, two_o), 0, moved
    )
    near = move_split(early, dx=1)
    (late,) = call(
        late_k,
        [((held, full), BF)],
        (targets, two, two_o, three, three_o, four, four_o),
        0,
        moved,
    )

    def choosing(groups, into, outs, pieces, first=()):
        def kernel(*refs):
            choose(rows, top, width, tile(full, 1664), groups, slots, into, *refs)

        return call(
            kernel,
            [((n, full), BF) for n in outs] + [((count, PAD), F32)] * 2,
            (targets, *pieces),
            2 * count * PAD * full * len(groups),
            4 * count * full * len(groups),
            first,
        )

    l0, l1, l2, l3, slot_l, ids_l = choosing(
        (1,), [[(d, 0) for d in range(NY)]], [slots] * NY, (late,)
    )
    l1, l2 = move(l1, dy=1), move(l2, dy=-1)

    def cut(targets, near, half, whole):
        m = half.shape[0]
        whole[...] = near[...]

        def fill(at):
            half[...] = near[at : at + m]

        pl.when(targets[NY] == 0)(lambda: fill(0))
        pl.when(targets[NY] == 1)(lambda: fill(m))

    half, near = call(
        cut,
        [((held // 2, full), BF), ((held, full), BF)],
        (targets, near),
        0,
        moved,
        (slot_l,),
    )
    far = move_split(half, dx=1)
    near_o, far_o = move(near, dc=1), move(far, dc=1)

    def join(*refs):
        *ins, out = refs
        for i, piece in enumerate(ins):
            out[i * slots : (i + 1) * slots] = piece[...]

    (late,) = call(
        join,
        [((NY * slots, full), BF)],
        (l0, l1, l2, move(l3, dy=2)),
        0,
        16 * slots * full,
        (far_o,),
    )
    late_near = both(late)
    all_x, part_x = 4 * slots, 2 * slots
    into = [
        [(0, x * slots), (1, x * slots), (2, x * slots), (1 + x // 2, all_x + x % 2 * slots)]
        for x in range(4)
    ]
    e0, e1, e2, slot_e, ids_e = choosing(
        (1, 1, 1, 2),
        into,
        [all_x, all_x + part_x, all_x + part_x],
        (early, near, near_o, far, far_o),
    )
    e1, e2 = move(e1, dy=1), move(e2, dy=-1)
    early_parts = [e0, e1, e2, move(e1[all_x:], dy=1), move(e2[all_x:], dy=-1)]
    early_sizes = [all_x] * 3 + [part_x] * 2
    late_far = onward(late_near)

    def back_and_forth(parts, sizes, per_x, first=()):
        def kernel(*refs):
            expert(top, tile(width, 1024), per_x, sizes, *refs)

        n = sum(sizes)
        r_own, r_left, r_right, r_fa, r_fb, hg, dg, du = call(
            kernel,
            [((n // 4, back_w), F32)]
            + [((n // 4, back_w), BF)] * 2
            + [((n // 8, back_w), BF)] * 2
            + [((n, share), BF)] * 3,
            (me, *parts, wg, wu, wd),
            2 * n * width * share * 5,
            2 * (n * full + n * back_w + 3 * share * width),
            first,
        )
        return (dg, du, hg), r_own, (r_left, r_right, r_fa, r_fb)

    def spans(many, n):
        near = [[(i * 4 * n + x * n, n) for i in range(many)] for x in range(4)]
        if many == 1:
            return near[:3] + [[(3 * n, n // 2)], [(3 * n + n // 2, n // 2)]]
        return near[:3] + [near[3][: many // 2], near[3][many // 2 :]]

    def returning(sums, forth):
        left, right, fa, fb = sums
        to_left, to_right = call(
            pass_on,
            [(left.shape, BF)] * 2,
            (left, right, forth(fa, 1), forth(fb, -1)),
            0,
            12 * left.size,
        )
        return forth(to_left, -1), forth(to_right, 1)

    def split_x(v, d):
        return move_split(v, dx=d)

    late_parts = [late, *late_near, *late_far]
    late_sizes = [p.shape[0] for p in late_parts]
    small_l, own_l, sums = back_and_forth(late_parts, late_sizes, spans(1, NY * slots))
    got_l = returning(sums, move_x)
    small_e, own_e, sums = back_and_forth(early_parts, early_sizes, spans(NY, slots), (own_l,))
    got_e = returning(sums, split_x)

    block = tile(width, 512)
    steps = width // block
    parts = [*late_parts, *early_parts]
    sizes = late_sizes + early_sizes
    small = [a for group in zip(small_l, small_e) for a in group]

    def outer_k(*refs):
        outer(len(parts), *refs)

    grad_gate, grad_up, grad_down = call(
        outer_k,
        [((share, width), BF)] * 3,
        parts + parts + small,
        2 * 3 * 8 * count * share * width,
        2 * (8 * count * full + 3 * share * width),
        got_l,
        grid=(steps,),
        in_specs=[pl.BlockSpec((n, block), lambda j: (0, j)) for n in sizes]
        + [pl.BlockSpec((n, block), lambda j: (0, j + steps)) for n in sizes]
        + [pl.BlockSpec(a.shape, lambda j: (0, 0)) for a in small],
        out_specs=[pl.BlockSpec((share, block), lambda j: (0, j))] * 3,
    )

    def home(own, got, first):
        h0, h1, h2, h3 = call(
            add_up,
            [((slots, back_w), BF)] * NY,
            (own, *got),
            0,
            20 * count * back_w,
            first,
        )
        return h0, move(h1, dy=-1), move(h2, dy=1), move(h3, dy=2)

    home_l = home(own_l, got_l, ())
    home_e = home(own_e, got_e, (grad_down,))

    def combine_k(*refs):
        combine(width, tile(width, 1024), *refs)

    keep, send = call(
        combine_k,
        [((count, back_w), F32), ((count, back_w), BF)],
        (targets, slot_e, ids_e, slot_l, ids_l, *home_e, *home_l),
        4 * count * count * back_w,
        10 * count * back_w,
    )
    cored = keep + move(send, dc=1).astype(F32)
    sent = cored.astype(BF)
    apart = sum(move_split(sent[i * n : (i + 1) * n], dz=i + 1).astype(F32) for i in range(3))
    opposite = move_split(sent[3 * n + rows :], dz=NZ // 2).astype(F32)
    ours = jnp.where(core == 0, apart[:rows], apart[rows:])
    theirs = jnp.where(core == 0, apart[rows:], apart[:rows])
    summed = cored[3 * n : 3 * n + rows] + opposite + ours
    summed = summed + move(theirs.astype(BF), dc=1).astype(F32)
    return (
        summed[:, :width].astype(BF),
        summed[:, width : width + top],
        grad_gate[None],
        grad_up[None],
        grad_down[None],
    )


def solution(mesh):
    both = P(("seq", "expert"), None)
    weight = P("expert", "seq", None)
    return jax.shard_map(
        body,
        mesh=mesh,
        in_specs=(both, both, both, both, weight, weight, weight),
        out_specs=(both, both, weight, weight, weight),
        check_vma=False,
    )
```

```python
import jax
import jax.numpy as jnp
from jax import lax
from jax.experimental import pallas as pl
from jax.experimental.pallas import tpu as pltpu
from jax.sharding import PartitionSpec as P

NY, NZ, NC = 4, 8, 2
Y_ORDER = (0, 1, -1, 2)
CAP = 2
PAD = 128
BF = jnp.bfloat16
F32 = jnp.float32
COLS = (((1,), (1,)), ((), ()))
ROWS = (((0,), (0,)), ((), ()))
ANY = pl.BlockSpec(memory_space=pl.ANY)
VMEM = pl.BlockSpec(memory_space=pltpu.VMEM)
SMEM = pl.BlockSpec(memory_space=pltpu.SMEM)


def dot(a, b, dims=(((1,), (0,)), ((), ()))):
    return lax.dot_general(a, b, dims, preferred_element_type=F32)


def tile(n, most):
    return max(b for b in range(PAD, most + 1, PAD) if n % b == 0)


def call(kernel, outs, args, flops, moved, first=(), mib=32, **more):
    specs = dict(
        in_specs=[SMEM if a.dtype == jnp.int32 else VMEM for a in args],
        out_specs=[VMEM] * len(outs),
    )
    specs.update(more)
    specs["in_specs"] = list(specs["in_specs"]) + [ANY] * len(first)
    count = len(args)

    def without(*refs):
        kernel(*refs[:count], *refs[count + len(first) :])

    return pl.pallas_call(
        without,
        out_shape=[jax.ShapeDtypeStruct(s, d) for s, d in outs],
        compiler_params=pltpu.CompilerParams(vmem_limit_bytes=mib * 2**20),
        cost_estimate=pl.CostEstimate(flops=flops, bytes_accessed=moved, transcendentals=0),
        **specs,
    )(*args, *first)


def move(v, dy=0, dz=0, dc=0):
    pairs = []
    for y in range(NY):
        for z in range(NZ):
            for c in range(NC):
                to = (((y + dy) % NY) * NZ + (z + dz) % NZ) * NC + (c + dc) % NC
                pairs.append(((y * NZ + z) * NC + c, to))
    return lax.ppermute(v, "expert", pairs)


def move_x(v, d):
    n = lax.axis_size("seq")
    return lax.ppermute(v, "seq", [(i, (i + d) % n) for i in range(n)])


def move_split(v, dx=0, dz=0):
    n = lax.axis_size("seq")
    pairs = []
    for x in range(n):
        for e in range(NY * NZ * NC):
            y, z, c = e // (NZ * NC), e // NC % NZ, e % NC
            sign = 1 - 2 * c
            to = (y * NZ + (z + sign * dz) % NZ) * NC + c
            pairs.append((x * NY * NZ * NC + e, (x + sign * dx) % n * NY * NZ * NC + to))
    return lax.ppermute(v, ("seq", "expert"), pairs)


def lanes(shape):
    return lax.broadcasted_iota(jnp.int32, shape, 1)


def one_hot(slot, slots):
    at = lanes(slot.shape)
    pick = jnp.zeros(slot.shape, F32)
    for d in range(NY):
        of = jnp.sum(jnp.where(at == d, slot, 0.0), axis=1, keepdims=True)
        pick = jnp.where(of == (at - d * slots).astype(F32), 1.0, pick)
    return pick.astype(BF)


def stacked(refs, cols):
    return jnp.concatenate([r[:, cols] for r in refs], axis=0) if len(refs) > 1 else refs[0][:, cols]


def choose(rows, top, width, block, groups, slots, into, targets, *refs):
    many = sum(groups)
    pieces, outs = refs[:many], refs[many:-2]
    slot_out, ids_out = refs[-2:]
    for g, n in enumerate(groups):
        mine, pieces = pieces[:n], pieces[n:]
        tail = stacked(mine, slice(2 * width, 2 * width + PAD)).astype(F32)
        count = tail.shape[0]
        at = lanes(tail.shape)
        row = lax.broadcasted_iota(jnp.int32, tail.shape, 0)
        ids = jnp.where(at < top, tail, -1.0)
        chosen = jnp.zeros(tail.shape, F32)
        for d in range(NY):
            hit = jnp.where(ids == targets[d].astype(F32), 1.0, 0.0)
            chosen = jnp.where(at == d, jnp.max(hit, axis=1, keepdims=True), chosen)
        r_at = lax.broadcasted_iota(jnp.int32, (count, count), 0)
        c_at = lanes((count, count))
        before = jnp.where((r_at // rows == c_at // rows) & (c_at < r_at), 1.0, 0.0).astype(BF)
        place = dot(before, chosen.astype(BF))
        first = row // rows * CAP
        if n == 2:
            first = (first + targets[NY] * (slots // 2)) % slots
        slot = jnp.where(chosen > 0.0, place + first.astype(F32), -4.0 * PAD)
        if g == 0:
            slot_out[...] = slot
            ids_out[...] = ids
        pick = one_hot(slot, slots)
        for j in range(0, 2 * width + PAD, block):
            part = dot(pick, stacked(mine, slice(j, j + block)), ROWS).astype(BF)
            for d in range(NY):
                out, at = into[g][d]
                outs[out][at : at + slots, j : j + block] = part[d * slots : (d + 1) * slots]


def expert(top, block, per_x, sizes, me, *refs):
    *pieces, wg, wu, wd, r_own, r_left, r_right, r_fa, r_fb, hg, dg, du = refs
    pieces = [p.at[:n] for p, n in zip(pieces, sizes)]
    width = wg.shape[1]
    tail = stacked(pieces, slice(2 * width, 2 * width + PAD)).astype(F32)
    gates = pltpu.roll(tail, PAD - top, 1)
    mask = (tail == me[0].astype(F32)) & (lanes(tail.shape) < top)
    gate = jnp.sum(jnp.where(mask, gates, 0.0), axis=1, keepdims=True)
    x = stacked(pieces, slice(0, width))
    pre_gate = dot(x, wg[...], COLS)
    pre_up = dot(x, wu[...], COLS)
    plain = dot(stacked(pieces, slice(width, 2 * width)), wd[...], COLS)
    sig = jax.nn.sigmoid(pre_gate)
    act = pre_gate * sig
    hidden = act * pre_up
    router = jnp.sum(hidden.astype(BF).astype(F32) * plain, axis=1, keepdims=True)
    grad_hidden = gate * plain
    d_gate = (grad_hidden * pre_up * (sig * (1.0 + pre_gate * (1.0 - sig)))).astype(BF)
    d_up = (grad_hidden * act).astype(BF)
    hg[...] = (gate * hidden).astype(BF)
    dg[...] = d_gate
    du[...] = d_up
    outs = (r_own, r_left, r_right, r_fa, r_fb)

    def put(cols, v):
        for out, spans in zip(outs, per_x):
            at = 0
            for start, n in spans:
                out[at : at + n, cols] = v[start : start + n].astype(out.dtype)
                at += n

    for j in range(0, width, block):
        cols = slice(j, j + block)
        put(cols, dot(d_gate, wg[:, cols]) + dot(d_up, wu[:, cols]))
    put(slice(width, width + PAD), jnp.broadcast_to(router, (router.shape[0], PAD)))


def pass_on(left, right, via_left, via_right, to_left, to_right):
    m = via_left.shape[0]
    to_left[:m] = left[:m]
    to_left[m:] = (left[m:].astype(F32) + via_right[...].astype(F32)).astype(BF)
    to_right[:m] = (right[:m].astype(F32) + via_left[...].astype(F32)).astype(BF)
    to_right[m:] = right[m:]


def add_up(mine, a, b, *outs):
    total = mine[...] + a[...].astype(F32) + b[...].astype(F32)
    slots = outs[0].shape[0]
    for d, out in enumerate(outs):
        out[...] = total[d * slots : (d + 1) * slots].astype(BF)


def combine(width, block, targets, slot_e, ids_e, slot_l, ids_l, e0, e1, e2, e3, l0, l1, l2, l3, keep, send):
    slots = l0.shape[0]
    n = keep.shape[0] // 4
    first = targets[NY] == 0
    narrow = [one_hot(slot[...], slots)[:, : NY * slots] for slot in (slot_e, slot_l)]
    homes = ((e0, e1, e2, e3), (l0, l1, l2, l3))

    def give(cols, e, l):
        e0, em1, ep1, em2 = (e[i * n : (i + 1) * n] for i in range(4))
        lp2, lm3, lp3, l4 = (l[i * n : (i + 1) * n] for i in range(4))
        plus = jnp.concatenate([ep1, lp2, lp3, e0[: n // 2], l4[: n // 2]], axis=0)
        minus = jnp.concatenate([em1, em2, lm3, e0[n // 2 :], l4[n // 2 :]], axis=0)
        keep[:, cols] = jnp.where(first, plus, minus)
        send[:, cols] = jnp.where(first, minus, plus).astype(BF)

    for j in range(0, width, block):
        cols = slice(j, j + block)
        give(cols, *(dot(p, stacked(home, cols)) for p, home in zip(narrow, homes)))
    tails = []
    for p, home, ids in zip(narrow, homes, (ids_e, ids_l)):
        tail = stacked(home, slice(width, width + PAD))
        at = lanes(p.shape)
        routed = jnp.zeros(ids.shape, F32)
        for d in range(NY):
            val = dot(jnp.where(at // slots == d, p, jnp.zeros_like(p)), tail)
            routed = routed + jnp.where(ids[...] == targets[d].astype(F32), val, 0.0)
        tails.append(routed)
    give(slice(width, width + PAD), *tails)


def outer(width, block, many, *refs):
    parts = refs[:many]
    *small, o_gate, o_up, o_down = refs[many:]
    third = len(small) // 3
    share = o_gate.shape[0]
    every = slice(None)

    def flip(group):
        return stacked(group, every).astype(F32).T.astype(BF)

    turned = jnp.concatenate([flip(small[:third]), flip(small[third : 2 * third])], axis=0)
    turned_h = flip(small[2 * third :])
    for j in range(0, width, block):
        both = dot(turned, stacked(parts, slice(j, j + block))).astype(BF)
        o_gate[:, j : j + block] = both[:share]
        o_up[:, j : j + block] = both[share:]
        y = stacked(parts, slice(width + j, width + j + block))
        o_down[:, j : j + block] = dot(turned_h, y).astype(BF)


def body(tokens, out_grad, expert_ids, gate_values, gate_weight, up_weight, down_weight):
    rows, width = tokens.shape
    top = expert_ids.shape[1]
    share = gate_weight.shape[1]
    full, back_w = 2 * width + PAD, width + PAD
    me = lax.axis_index("expert").astype(jnp.int32)
    my_y, my_zc = me // (NZ * NC), me % (NZ * NC)
    core = me % NC
    targets = jnp.stack([((my_y + d) % NY) * (NZ * NC) + my_zc for d in Y_ORDER] + [core])
    me = me[None]
    wg, wu, wd = gate_weight[0], up_weight[0], down_weight[0]

    extra = jnp.concatenate(
        [expert_ids.astype(BF), gate_values, jnp.zeros((rows, PAD - 2 * top), BF)], axis=1
    )
    pay = jnp.concatenate([tokens, out_grad, extra], axis=1)

    def both(v):
        return move_x(v, 1), move_x(v, -1)

    def onward(near):
        n = near[0].shape[0] // 2
        return move_x(near[0][:n], 1), move_x(near[1][n:], -1)

    across = move(pay, dc=1)
    pair = jnp.concatenate(
        [jnp.where(core == 0, pay, across), jnp.where(core == 0, across, pay)], axis=0
    )
    one, two = move_split(pair, dz=1), move_split(pair, dz=2)
    three = move_split(two, dz=1)
    four = move_split(lax.dynamic_slice_in_dim(two, core * width, width + PAD, 1), dz=2)
    one_o, two_o, three_o, four_o = (move(v, dc=1) for v in (one, two, three, four))
    n = NC * rows
    held = 4 * n
    count = held
    slots = count // rows * CAP

    def early_k(targets, pair, one, one_o, two, two_o, out):
        out[:n] = pair[...]

        def fill(minus, plus, last):
            out[n : 2 * n] = minus[...]
            out[2 * n : 3 * n] = plus[...]
            out[3 * n :] = last[...]

        pl.when(targets[NY] == 0)(lambda: fill(one, one_o, two))
        pl.when(targets[NY] == 1)(lambda: fill(one_o, one, two_o))

    def late_k(targets, two, two_o, three, three_o, four, four_o, out):
        def fill(plus2, minus3, plus3, low, high):
            out[:n] = plus2[...]
            out[n : 2 * n] = minus3[...]
            out[2 * n : 3 * n] = plus3[...]
            out[3 * n :, : width + PAD] = low[...]
            out[3 * n :, width:] = high[...]

        pl.when(targets[NY] == 0)(lambda: fill(two_o, three, three_o, four, four_o))
        pl.when(targets[NY] == 1)(lambda: fill(two, three_o, three, four_o, four))

    moved = 4 * held * full
    (early,) = call(
        early_k, [((held, full), BF)], (targets, pair, one, one_o, two, two_o), 0, moved
    )
    near = move_split(early, dx=1)
    (late,) = call(
        late_k,
        [((held, full), BF)],
        (targets, two, two_o, three, three_o, four, four_o),
        0,
        moved,
    )

    def choosing(groups, into, outs, pieces, first=()):
        def kernel(*refs):
            choose(rows, top, width, tile(full, 1664), groups, slots, into, *refs)

        return call(
            kernel,
            [((n, full), BF) for n in outs] + [((count, PAD), F32)] * 2,
            (targets, *pieces),
            2 * count * PAD * full * len(groups),
            4 * count * full * len(groups),
            first,
        )

    l0, l1, l2, l3, slot_l, ids_l = choosing(
        (1,), [[(d, 0) for d in range(NY)]], [slots] * NY, (late,)
    )
    l1, l2, l3 = move(l1, dy=1), move(l2, dy=-1), move(l3, dy=2)

    def cut(targets, near, half, whole):
        m = half.shape[0]
        whole[...] = near[...]

        def fill(at):
            half[...] = near[at : at + m]

        pl.when(targets[NY] == 0)(lambda: fill(0))
        pl.when(targets[NY] == 1)(lambda: fill(m))

    half, near = call(
        cut,
        [((held // 2, full), BF), ((held, full), BF)],
        (targets, near),
        0,
        moved,
        (slot_l,),
    )
    far = move_split(half, dx=1)

    def hold(far, out):
        out[...] = far[...]

    (far,) = call(hold, [(far.shape, BF)], (far,), 0, moved, (l1, l2, l3))
    near_o, far_o = move(near, dc=1), move(far, dc=1)

    def join(*refs):
        *ins, out = refs
        for i, piece in enumerate(ins):
            out[i * slots : (i + 1) * slots] = piece[...]

    (late,) = call(
        join,
        [((NY * slots, full), BF)],
        (l0, l1, l2, l3),
        0,
        16 * slots * full,
        (far_o,),
    )
    late_near = both(late)
    all_x, part_x = 4 * slots, 2 * slots
    into = [
        [(0, x * slots), (1, x * slots), (2, x * slots), (1 + x // 2, all_x + x % 2 * slots)]
        for x in range(4)
    ]
    e0, e1, e2, slot_e, ids_e = choosing(
        (1, 1, 1, 2),
        into,
        [all_x, all_x + part_x, all_x + part_x],
        (early, near, near_o, far, far_o),
    )
    e1, e2 = move(e1, dy=1), move(e2, dy=-1)
    early_parts = [e0, e1, e2, move(e1[all_x:], dy=1), move(e2[all_x:], dy=-1)]
    early_sizes = [all_x] * 3 + [part_x] * 2
    late_far = onward(late_near)

    def back_and_forth(parts, sizes, per_x, first=()):
        def kernel(*refs):
            expert(top, tile(width, 1024), per_x, sizes, *refs)

        n = sum(sizes)
        r_own, r_left, r_right, r_fa, r_fb, hg, dg, du = call(
            kernel,
            [((n // 4, back_w), F32)]
            + [((n // 4, back_w), BF)] * 2
            + [((n // 8, back_w), BF)] * 2
            + [((n, share), BF)] * 3,
            (me, *parts, wg, wu, wd),
            2 * n * width * share * 5,
            2 * (n * full + n * back_w + 3 * share * width),
            first,
        )
        return (dg, du, hg), r_own, (r_left, r_right, r_fa, r_fb)

    def spans(many, n):
        near = [[(i * 4 * n + x * n, n) for i in range(many)] for x in range(4)]
        if many == 1:
            return near[:3] + [[(3 * n, n // 2)], [(3 * n + n // 2, n // 2)]]
        return near[:3] + [near[3][: many // 2], near[3][many // 2 :]]

    def returning(sums, forth):
        left, right, fa, fb = sums
        to_left, to_right = call(
            pass_on,
            [(left.shape, BF)] * 2,
            (left, right, forth(fa, 1), forth(fb, -1)),
            0,
            12 * left.size,
        )
        return forth(to_left, -1), forth(to_right, 1)

    def split_x(v, d):
        return move_split(v, dx=d)

    late_parts = [late, *late_near, *late_far]
    late_sizes = [p.shape[0] for p in late_parts]
    small_l, own_l, sums = back_and_forth(late_parts, late_sizes, spans(1, NY * slots))
    got_l = returning(sums, move_x)
    small_e, own_e, sums = back_and_forth(early_parts, early_sizes, spans(NY, slots), (own_l,))
    got_e = returning(sums, split_x)

    sizes = late_sizes + early_sizes
    small = [a for group in zip(small_l, small_e) for a in group]

    def outer_k(*refs):
        parts = [p.at[:n] for p, n in zip(refs, sizes)]
        outer(width, tile(width, 512), len(sizes), *parts, *refs[len(sizes) :])

    grad_gate, grad_up, grad_down = call(
        outer_k,
        [((share, width), BF)] * 3,
        (*late_parts, *early_parts, *small),
        2 * 3 * 8 * count * share * width,
        2 * (8 * count * full + 3 * share * width),
        got_l,
    )

    def home(own, got, first):
        h0, h1, h2, h3 = call(
            add_up,
            [((slots, back_w), BF)] * NY,
            (own, *got),
            0,
            20 * count * back_w,
            first,
        )
        return h0, move(h1, dy=-1), move(h2, dy=1), move(h3, dy=2)

    home_l = home(own_l, got_l, ())
    home_e = home(own_e, got_e, (grad_down,))

    def combine_k(*refs):
        combine(width, tile(width, 1024), *refs)

    keep, send = call(
        combine_k,
        [((count, back_w), F32), ((count, back_w), BF)],
        (targets, slot_e, ids_e, slot_l, ids_l, *home_e, *home_l),
        4 * count * count * back_w,
        10 * count * back_w,
    )
    cored = keep + move(send, dc=1).astype(F32)
    sent = cored.astype(BF)
    apart = sum(move_split(sent[i * n : (i + 1) * n], dz=i + 1).astype(F32) for i in range(3))
    opposite = move_split(sent[3 * n + rows :], dz=NZ // 2).astype(F32)
    ours = jnp.where(core == 0, apart[:rows], apart[rows:])
    theirs = jnp.where(core == 0, apart[rows:], apart[:rows])
    summed = cored[3 * n : 3 * n + rows] + opposite + ours
    summed = summed + move(theirs.astype(BF), dc=1).astype(F32)
    return (
        summed[:, :width].astype(BF),
        summed[:, width : width + top],
        grad_gate[None],
        grad_up[None],
        grad_down[None],
    )


def solution(mesh):
    both = P(("seq", "expert"), None)
    weight = P("expert", "seq", None)
    return jax.shard_map(
        body,
        mesh=mesh,
        in_specs=(both, both, both, both, weight, weight, weight),
        out_specs=(both, both, weight, weight, weight),
        check_vma=False,
    )
```

```python
import jax
import jax.numpy as jnp
from jax import lax
from jax.experimental import pallas as pl
from jax.experimental.pallas import tpu as pltpu
from jax.sharding import PartitionSpec as P

NY, NZ, NC = 4, 8, 2
Y_ORDER = (0, 1, -1, 2)
CAP = 2
PAD = 128
BF = jnp.bfloat16
F32 = jnp.float32
COLS = (((1,), (1,)), ((), ()))
ROWS = (((0,), (0,)), ((), ()))
ANY = pl.BlockSpec(memory_space=pl.ANY)
VMEM = pl.BlockSpec(memory_space=pltpu.VMEM)
SMEM = pl.BlockSpec(memory_space=pltpu.SMEM)


def dot(a, b, dims=(((1,), (0,)), ((), ()))):
    return lax.dot_general(a, b, dims, preferred_element_type=F32)


def tile(n, most):
    return max(b for b in range(PAD, most + 1, PAD) if n % b == 0)


def call(kernel, outs, args, flops, moved, first=(), mib=32, **more):
    specs = dict(
        in_specs=[SMEM if a.dtype == jnp.int32 else VMEM for a in args],
        out_specs=[VMEM] * len(outs),
    )
    specs.update(more)
    specs["in_specs"] = list(specs["in_specs"]) + [ANY] * len(first)
    count = len(args)

    def without(*refs):
        kernel(*refs[:count], *refs[count + len(first) :])

    return pl.pallas_call(
        without,
        out_shape=[jax.ShapeDtypeStruct(s, d) for s, d in outs],
        compiler_params=pltpu.CompilerParams(vmem_limit_bytes=mib * 2**20),
        cost_estimate=pl.CostEstimate(flops=flops, bytes_accessed=moved, transcendentals=0),
        **specs,
    )(*args, *first)


def move(v, dy=0, dz=0, dc=0):
    pairs = []
    for y in range(NY):
        for z in range(NZ):
            for c in range(NC):
                to = (((y + dy) % NY) * NZ + (z + dz) % NZ) * NC + (c + dc) % NC
                pairs.append(((y * NZ + z) * NC + c, to))
    return lax.ppermute(v, "expert", pairs)


def move_x(v, d):
    n = lax.axis_size("seq")
    return lax.ppermute(v, "seq", [(i, (i + d) % n) for i in range(n)])


def move_split(v, dx=0, dz=0):
    n = lax.axis_size("seq")
    pairs = []
    for x in range(n):
        for e in range(NY * NZ * NC):
            y, z, c = e // (NZ * NC), e // NC % NZ, e % NC
            sign = 1 - 2 * c
            to = (y * NZ + (z + sign * dz) % NZ) * NC + c
            pairs.append((x * NY * NZ * NC + e, (x + sign * dx) % n * NY * NZ * NC + to))
    return lax.ppermute(v, ("seq", "expert"), pairs)


def lanes(shape):
    return lax.broadcasted_iota(jnp.int32, shape, 1)


def one_hot(slot, slots):
    at = lanes(slot.shape)
    pick = jnp.zeros(slot.shape, F32)
    for d in range(NY):
        of = jnp.sum(jnp.where(at == d, slot, 0.0), axis=1, keepdims=True)
        pick = jnp.where(of == (at - d * slots).astype(F32), 1.0, pick)
    return pick.astype(BF)


def stacked(refs, cols):
    return jnp.concatenate([r[:, cols] for r in refs], axis=0) if len(refs) > 1 else refs[0][:, cols]


def choose(rows, top, width, block, groups, slots, into, targets, *refs):
    many = sum(groups)
    pieces, outs = refs[:many], refs[many:-2]
    slot_out, ids_out = refs[-2:]
    for g, n in enumerate(groups):
        mine, pieces = pieces[:n], pieces[n:]
        tail = stacked(mine, slice(2 * width, 2 * width + PAD)).astype(F32)
        count = tail.shape[0]
        at = lanes(tail.shape)
        row = lax.broadcasted_iota(jnp.int32, tail.shape, 0)
        ids = jnp.where(at < top, tail, -1.0)
        chosen = jnp.zeros(tail.shape, F32)
        for d in range(NY):
            hit = jnp.where(ids == targets[d].astype(F32), 1.0, 0.0)
            chosen = jnp.where(at == d, jnp.max(hit, axis=1, keepdims=True), chosen)
        r_at = lax.broadcasted_iota(jnp.int32, (count, count), 0)
        c_at = lanes((count, count))
        before = jnp.where((r_at // rows == c_at // rows) & (c_at < r_at), 1.0, 0.0).astype(BF)
        place = dot(before, chosen.astype(BF))
        first = row // rows * CAP
        if n == 2:
            first = (first + targets[NY] * (slots // 2)) % slots
        slot = jnp.where(chosen > 0.0, place + first.astype(F32), -4.0 * PAD)
        if g == 0:
            slot_out[...] = slot
            ids_out[...] = ids
        pick = one_hot(slot, slots)[:, : NY * slots]
        for j in range(0, 2 * width + PAD, block):
            part = dot(pick, stacked(mine, slice(j, j + block)), ROWS).astype(BF)
            for d in range(NY):
                out, at = into[g][d]
                outs[out][at : at + slots, j : j + block] = part[d * slots : (d + 1) * slots]


def expert(top, block, per_x, sizes, me, *refs):
    *pieces, wg, wu, wd, r_own, r_left, r_right, r_fa, r_fb, hg, dg, du = refs
    pieces = [p.at[:n] for p, n in zip(pieces, sizes)]
    width = wg.shape[1]
    tail = stacked(pieces, slice(2 * width, 2 * width + PAD)).astype(F32)
    gates = pltpu.roll(tail, PAD - top, 1)
    mask = (tail == me[0].astype(F32)) & (lanes(tail.shape) < top)
    gate = jnp.sum(jnp.where(mask, gates, 0.0), axis=1, keepdims=True)
    x = stacked(pieces, slice(0, width))
    pre_gate = dot(x, wg[...], COLS)
    pre_up = dot(x, wu[...], COLS)
    plain = dot(stacked(pieces, slice(width, 2 * width)), wd[...], COLS)
    sig = jax.nn.sigmoid(pre_gate)
    act = pre_gate * sig
    hidden = act * pre_up
    router = jnp.sum(hidden.astype(BF).astype(F32) * plain, axis=1, keepdims=True)
    grad_hidden = gate * plain
    d_gate = (grad_hidden * pre_up * (sig * (1.0 + pre_gate * (1.0 - sig)))).astype(BF)
    d_up = (grad_hidden * act).astype(BF)
    hg[...] = (gate * hidden).astype(BF)
    dg[...] = d_gate
    du[...] = d_up
    outs = (r_own, r_left, r_right, r_fa, r_fb)

    def put(cols, v):
        for out, spans in zip(outs, per_x):
            at = 0
            for start, n in spans:
                out[at : at + n, cols] = v[start : start + n].astype(out.dtype)
                at += n

    for j in range(0, width, block):
        cols = slice(j, j + block)
        put(cols, dot(d_gate, wg[:, cols]) + dot(d_up, wu[:, cols]))
    put(slice(width, width + PAD), jnp.broadcast_to(router, (router.shape[0], PAD)))


def pass_on(left, right, via_left, via_right, to_left, to_right):
    m = via_left.shape[0]
    to_left[:m] = left[:m]
    to_left[m:] = (left[m:].astype(F32) + via_right[...].astype(F32)).astype(BF)
    to_right[:m] = (right[:m].astype(F32) + via_left[...].astype(F32)).astype(BF)
    to_right[m:] = right[m:]


def add_up(mine, a, b, *outs):
    total = mine[...] + a[...].astype(F32) + b[...].astype(F32)
    slots = outs[0].shape[0]
    for d, out in enumerate(outs):
        out[...] = total[d * slots : (d + 1) * slots].astype(BF)


def combine(width, block, targets, slot_e, ids_e, slot_l, ids_l, e0, e1, e2, e3, l0, l1, l2, l3, keep, send):
    slots = l0.shape[0]
    n = keep.shape[0] // 4
    first = targets[NY] == 0
    narrow = [one_hot(slot[...], slots)[:, : NY * slots] for slot in (slot_e, slot_l)]
    homes = ((e0, e1, e2, e3), (l0, l1, l2, l3))

    def give(cols, e, l):
        e0, em1, ep1, em2 = (e[i * n : (i + 1) * n] for i in range(4))
        lp2, lm3, lp3, l4 = (l[i * n : (i + 1) * n] for i in range(4))
        plus = jnp.concatenate([ep1, lp2, lp3, e0[: n // 2], l4[: n // 2]], axis=0)
        minus = jnp.concatenate([em1, em2, lm3, e0[n // 2 :], l4[n // 2 :]], axis=0)
        keep[:, cols] = jnp.where(first, plus, minus)
        send[:, cols] = jnp.where(first, minus, plus).astype(BF)

    for j in range(0, width, block):
        cols = slice(j, j + block)
        give(cols, *(dot(p, stacked(home, cols)) for p, home in zip(narrow, homes)))
    tails = []
    for p, home, ids in zip(narrow, homes, (ids_e, ids_l)):
        tail = stacked(home, slice(width, width + PAD))
        at = lanes(p.shape)
        routed = jnp.zeros(ids.shape, F32)
        for d in range(NY):
            val = dot(jnp.where(at // slots == d, p, jnp.zeros_like(p)), tail)
            routed = routed + jnp.where(ids[...] == targets[d].astype(F32), val, 0.0)
        tails.append(routed)
    give(slice(width, width + PAD), *tails)


def outer(width, block, many, *refs):
    parts = refs[:many]
    *small, o_gate, o_up, o_down, ready = refs[many:]
    third = len(small) // 3
    share = o_gate.shape[0]
    ready[...] = jnp.zeros(ready.shape, F32)
    every = slice(None)

    def flip(group):
        return stacked(group, every).astype(F32).T.astype(BF)

    turned = jnp.concatenate([flip(small[:third]), flip(small[third : 2 * third])], axis=0)
    turned_h = flip(small[2 * third :])
    for j in range(0, width, block):
        both = dot(turned, stacked(parts, slice(j, j + block))).astype(BF)
        o_gate[:, j : j + block] = both[:share]
        o_up[:, j : j + block] = both[share:]
        y = stacked(parts, slice(width + j, width + j + block))
        o_down[:, j : j + block] = dot(turned_h, y).astype(BF)


def body(tokens, out_grad, expert_ids, gate_values, gate_weight, up_weight, down_weight):
    rows, width = tokens.shape
    top = expert_ids.shape[1]
    share = gate_weight.shape[1]
    full, back_w = 2 * width + PAD, width + PAD
    me = lax.axis_index("expert").astype(jnp.int32)
    my_y, my_zc = me // (NZ * NC), me % (NZ * NC)
    core = me % NC
    targets = jnp.stack([((my_y + d) % NY) * (NZ * NC) + my_zc for d in Y_ORDER] + [core])
    me = me[None]
    wg, wu, wd = gate_weight[0], up_weight[0], down_weight[0]

    extra = jnp.concatenate(
        [expert_ids.astype(BF), gate_values, jnp.zeros((rows, PAD - 2 * top), BF)], axis=1
    )
    pay = jnp.concatenate([tokens, out_grad, extra], axis=1)

    def both(v):
        return move_x(v, 1), move_x(v, -1)

    def onward(near):
        n = near[0].shape[0] // 2
        return move_x(near[0][:n], 1), move_x(near[1][n:], -1)

    across = move(pay, dc=1)
    pair = jnp.concatenate(
        [jnp.where(core == 0, pay, across), jnp.where(core == 0, across, pay)], axis=0
    )
    one, two = move_split(pair, dz=1), move_split(pair, dz=2)
    three = move_split(two, dz=1)
    four = move_split(lax.dynamic_slice_in_dim(two, core * width, width + PAD, 1), dz=2)
    one_o, two_o, three_o, four_o = (move(v, dc=1) for v in (one, two, three, four))
    n = NC * rows
    held = 4 * n
    count = held
    slots = count // rows * CAP

    def early_k(targets, pair, one, one_o, two, two_o, out):
        out[:n] = pair[...]

        def fill(minus, plus, last):
            out[n : 2 * n] = minus[...]
            out[2 * n : 3 * n] = plus[...]
            out[3 * n :] = last[...]

        pl.when(targets[NY] == 0)(lambda: fill(one, one_o, two))
        pl.when(targets[NY] == 1)(lambda: fill(one_o, one, two_o))

    def late_k(targets, two, two_o, three, three_o, four, four_o, out):
        def fill(plus2, minus3, plus3, low, high):
            out[:n] = plus2[...]
            out[n : 2 * n] = minus3[...]
            out[2 * n : 3 * n] = plus3[...]
            out[3 * n :, : width + PAD] = low[...]
            out[3 * n :, width:] = high[...]

        pl.when(targets[NY] == 0)(lambda: fill(two_o, three, three_o, four, four_o))
        pl.when(targets[NY] == 1)(lambda: fill(two, three_o, three, four_o, four))

    moved = 4 * held * full
    (early,) = call(
        early_k, [((held, full), BF)], (targets, pair, one, one_o, two, two_o), 0, moved
    )
    near = move_split(early, dx=1)
    (late,) = call(
        late_k,
        [((held, full), BF)],
        (targets, two, two_o, three, three_o, four, four_o),
        0,
        moved,
    )

    def choosing(groups, into, outs, pieces, first=()):
        def kernel(*refs):
            choose(rows, top, width, tile(full, 1664), groups, slots, into, *refs)

        return call(
            kernel,
            [((n, full), BF) for n in outs] + [((count, PAD), F32)] * 2,
            (targets, *pieces),
            2 * count * PAD * full * len(groups),
            4 * count * full * len(groups),
            first,
        )

    l0, l1, l2, l3, slot_l, ids_l = choosing(
        (1,), [[(d, 0) for d in range(NY)]], [slots] * NY, (late,)
    )
    l1, l2, l3 = move(l1, dy=1), move(l2, dy=-1), move(l3, dy=2)

    def cut(targets, near, half, whole):
        m = half.shape[0]
        whole[...] = near[...]

        def fill(at):
            half[...] = near[at : at + m]

        pl.when(targets[NY] == 0)(lambda: fill(0))
        pl.when(targets[NY] == 1)(lambda: fill(m))

    half, near = call(
        cut,
        [((held // 2, full), BF), ((held, full), BF)],
        (targets, near),
        0,
        moved,
        (slot_l,),
    )
    far = move_split(half, dx=1)

    def hold(far, out):
        out[...] = far[...]

    (far,) = call(hold, [(far.shape, BF)], (far,), 0, moved, (l1, l2, l3))
    near_o, far_o = move(near, dc=1), move(far, dc=1)

    def join(*refs):
        *ins, out = refs
        for i, piece in enumerate(ins):
            out[i * slots : (i + 1) * slots] = piece[...]

    (late,) = call(
        join,
        [((NY * slots, full), BF)],
        (l0, l1, l2, l3),
        0,
        16 * slots * full,
        (far_o,),
    )
    late_near = both(late)
    all_x, part_x = 4 * slots, 2 * slots
    into = [
        [(0, x * slots), (1, x * slots), (2, x * slots), (1 + x // 2, all_x + x % 2 * slots)]
        for x in range(4)
    ]
    e0, e1, e2, slot_e, ids_e = choosing(
        (1, 1, 1, 2),
        into,
        [all_x, all_x + part_x, all_x + part_x],
        (early, near, near_o, far, far_o),
    )
    e1, e2 = move(e1, dy=1), move(e2, dy=-1)
    early_parts = [e0, e1, e2, move(e1[all_x:], dy=1), move(e2[all_x:], dy=-1)]
    early_sizes = [all_x] * 3 + [part_x] * 2
    late_far = onward(late_near)

    def back_and_forth(parts, sizes, per_x, first=()):
        def kernel(*refs):
            expert(top, tile(width, 1024), per_x, sizes, *refs)

        n = sum(sizes)
        r_own, r_left, r_right, r_fa, r_fb, hg, dg, du = call(
            kernel,
            [((n // 4, back_w), F32)]
            + [((n // 4, back_w), BF)] * 2
            + [((n // 8, back_w), BF)] * 2
            + [((n, share), BF)] * 3,
            (me, *parts, wg, wu, wd),
            2 * n * width * share * 5,
            2 * (n * full + n * back_w + 3 * share * width),
            first,
        )
        return (dg, du, hg), r_own, (r_left, r_right, r_fa, r_fb)

    def spans(many, n):
        near = [[(i * 4 * n + x * n, n) for i in range(many)] for x in range(4)]
        if many == 1:
            return near[:3] + [[(3 * n, n // 2)], [(3 * n + n // 2, n // 2)]]
        return near[:3] + [near[3][: many // 2], near[3][many // 2 :]]

    def returning(sums, forth):
        left, right, fa, fb = sums
        to_left, to_right = call(
            pass_on,
            [(left.shape, BF)] * 2,
            (left, right, forth(fa, 1), forth(fb, -1)),
            0,
            12 * left.size,
        )
        return forth(to_left, -1), forth(to_right, 1)

    def split_x(v, d):
        return move_split(v, dx=d)

    late_parts = [late, *late_near, *late_far]
    late_sizes = [p.shape[0] for p in late_parts]
    small_l, own_l, sums = back_and_forth(late_parts, late_sizes, spans(1, NY * slots))
    got_l = returning(sums, move_x)
    small_e, own_e, sums = back_and_forth(early_parts, early_sizes, spans(NY, slots), (own_l,))
    got_e = returning(sums, split_x)

    sizes = late_sizes + early_sizes
    small = [a for group in zip(small_l, small_e) for a in group]

    def outer_k(*refs):
        parts = [p.at[:n] for p, n in zip(refs, sizes)]
        outer(width, tile(width, 512), len(sizes), *parts, *refs[len(sizes) :])

    grad_gate, grad_up, grad_down, ready = call(
        outer_k,
        [((share, width), BF)] * 3 + [((8, PAD), F32)],
        (*late_parts, *early_parts, *small),
        2 * 3 * 8 * count * share * width,
        2 * (8 * count * full + 3 * share * width),
        got_l,
    )

    def home(own, got, first):
        h0, h1, h2, h3 = call(
            add_up,
            [((slots, back_w), BF)] * NY,
            (own, *got),
            0,
            20 * count * back_w,
            first,
        )
        return h0, move(h1, dy=-1), move(h2, dy=1), move(h3, dy=2)

    home_l = home(own_l, got_l, ())
    home_e = home(own_e, got_e, (ready,))

    def combine_k(*refs):
        combine(width, tile(width, 1024), *refs)

    keep, send = call(
        combine_k,
        [((count, back_w), F32), ((count, back_w), BF)],
        (targets, slot_e, ids_e, slot_l, ids_l, *home_e, *home_l),
        4 * count * count * back_w,
        10 * count * back_w,
    )
    cored = keep + move(send, dc=1).astype(F32)
    sent = cored.astype(BF)
    apart = sum(move_split(sent[i * n : (i + 1) * n], dz=i + 1).astype(F32) for i in range(3))
    opposite = move_split(sent[3 * n + rows :], dz=NZ // 2).astype(F32)
    ours = jnp.where(core == 0, apart[:rows], apart[rows:])
    theirs = jnp.where(core == 0, apart[rows:], apart[:rows])
    summed = cored[3 * n : 3 * n + rows] + opposite + ours
    summed = summed + move(theirs.astype(BF), dc=1).astype(F32)
    return (
        summed[:, :width].astype(BF),
        summed[:, width : width + top],
        grad_gate[None],
        grad_up[None],
        grad_down[None],
    )


def solution(mesh):
    both = P(("seq", "expert"), None)
    weight = P("expert", "seq", None)
    return jax.shard_map(
        body,
        mesh=mesh,
        in_specs=(both, both, both, both, weight, weight, weight),
        out_specs=(both, both, weight, weight, weight),
        check_vma=False,
    )
```

```python
import jax
import jax.numpy as jnp
from jax import lax
from jax.experimental import pallas as pl
from jax.experimental.pallas import tpu as pltpu
from jax.sharding import PartitionSpec as P

NY, NZ, NC = 4, 8, 2
Y_ORDER = (0, 1, -1, 2)
CAP = 2
PAD = 128
BF = jnp.bfloat16
F32 = jnp.float32
COLS = (((1,), (1,)), ((), ()))
ROWS = (((0,), (0,)), ((), ()))
ANY = pl.BlockSpec(memory_space=pl.ANY)
VMEM = pl.BlockSpec(memory_space=pltpu.VMEM)
SMEM = pl.BlockSpec(memory_space=pltpu.SMEM)


def dot(a, b, dims=(((1,), (0,)), ((), ()))):
    return lax.dot_general(a, b, dims, preferred_element_type=F32)


def tile(n, most):
    return max(b for b in range(PAD, most + 1, PAD) if n % b == 0)


def call(kernel, outs, args, flops, moved, first=(), mib=32, **more):
    specs = dict(
        in_specs=[SMEM if a.dtype == jnp.int32 else VMEM for a in args],
        out_specs=[VMEM] * len(outs),
    )
    specs.update(more)
    specs["in_specs"] = list(specs["in_specs"]) + [ANY] * len(first)
    count = len(args)

    def without(*refs):
        kernel(*refs[:count], *refs[count + len(first) :])

    return pl.pallas_call(
        without,
        out_shape=[jax.ShapeDtypeStruct(s, d) for s, d in outs],
        compiler_params=pltpu.CompilerParams(vmem_limit_bytes=mib * 2**20),
        cost_estimate=pl.CostEstimate(flops=flops, bytes_accessed=moved, transcendentals=0),
        **specs,
    )(*args, *first)


def move(v, dy=0, dz=0, dc=0):
    pairs = []
    for y in range(NY):
        for z in range(NZ):
            for c in range(NC):
                to = (((y + dy) % NY) * NZ + (z + dz) % NZ) * NC + (c + dc) % NC
                pairs.append(((y * NZ + z) * NC + c, to))
    return lax.ppermute(v, "expert", pairs)


def move_x(v, d):
    n = lax.axis_size("seq")
    return lax.ppermute(v, "seq", [(i, (i + d) % n) for i in range(n)])


def move_split(v, dx=0, dz=0):
    n = lax.axis_size("seq")
    pairs = []
    for x in range(n):
        for e in range(NY * NZ * NC):
            y, z, c = e // (NZ * NC), e // NC % NZ, e % NC
            sign = 1 - 2 * c
            to = (y * NZ + (z + sign * dz) % NZ) * NC + c
            pairs.append((x * NY * NZ * NC + e, (x + sign * dx) % n * NY * NZ * NC + to))
    return lax.ppermute(v, ("seq", "expert"), pairs)


def lanes(shape):
    return lax.broadcasted_iota(jnp.int32, shape, 1)


def one_hot(slot, slots):
    at = lanes(slot.shape)
    pick = jnp.zeros(slot.shape, F32)
    for d in range(NY):
        of = jnp.sum(jnp.where(at == d, slot, 0.0), axis=1, keepdims=True)
        pick = jnp.where(of == (at - d * slots).astype(F32), 1.0, pick)
    return pick.astype(BF)


def stacked(refs, cols):
    return jnp.concatenate([r[:, cols] for r in refs], axis=0) if len(refs) > 1 else refs[0][:, cols]


def choose(rows, top, width, block, groups, slots, into, targets, *refs):
    many = sum(groups)
    pieces, outs = refs[:many], refs[many:-2]
    slot_out, ids_out = refs[-2:]
    for g, n in enumerate(groups):
        mine, pieces = pieces[:n], pieces[n:]
        tail = stacked(mine, slice(2 * width, 2 * width + PAD)).astype(F32)
        count = tail.shape[0]
        at = lanes(tail.shape)
        row = lax.broadcasted_iota(jnp.int32, tail.shape, 0)
        ids = jnp.where(at < top, tail, -1.0)
        chosen = jnp.zeros(tail.shape, F32)
        for d in range(NY):
            hit = jnp.where(ids == targets[d].astype(F32), 1.0, 0.0)
            chosen = jnp.where(at == d, jnp.max(hit, axis=1, keepdims=True), chosen)
        r_at = lax.broadcasted_iota(jnp.int32, (count, count), 0)
        c_at = lanes((count, count))
        before = jnp.where((r_at // rows == c_at // rows) & (c_at < r_at), 1.0, 0.0).astype(BF)
        place = dot(before, chosen.astype(BF))
        first = row // rows * CAP
        if n == 2:
            first = (first + targets[NY] * (slots // 2)) % slots
        slot = jnp.where(chosen > 0.0, place + first.astype(F32), -4.0 * PAD)
        if g == 0:
            slot_out[...] = slot
            ids_out[...] = ids
        pick = one_hot(slot, slots)[:, : NY * slots]
        for j in range(0, 2 * width + PAD, block):
            part = dot(pick, stacked(mine, slice(j, j + block)), ROWS).astype(BF)
            for d in range(NY):
                out, at = into[g][d]
                outs[out][at : at + slots, j : j + block] = part[d * slots : (d + 1) * slots]


def expert(top, block, per_x, sizes, me, *refs):
    *pieces, wg, wu, wd, r_own, r_left, r_right, r_fa, r_fb, hg, dg, du = refs
    pieces = [p.at[:n] for p, n in zip(pieces, sizes)]
    width = wg.shape[1]
    tail = stacked(pieces, slice(2 * width, 2 * width + PAD)).astype(F32)
    gates = pltpu.roll(tail, PAD - top, 1)
    mask = (tail == me[0].astype(F32)) & (lanes(tail.shape) < top)
    gate = jnp.sum(jnp.where(mask, gates, 0.0), axis=1, keepdims=True)
    x = stacked(pieces, slice(0, width))
    pre_gate = dot(x, wg[...], COLS)
    pre_up = dot(x, wu[...], COLS)
    plain = dot(stacked(pieces, slice(width, 2 * width)), wd[...], COLS)
    sig = jax.nn.sigmoid(pre_gate)
    act = pre_gate * sig
    hidden = act * pre_up
    router = jnp.sum(hidden.astype(BF).astype(F32) * plain, axis=1, keepdims=True)
    grad_hidden = gate * plain
    d_gate = (grad_hidden * pre_up * (sig * (1.0 + pre_gate * (1.0 - sig)))).astype(BF)
    d_up = (grad_hidden * act).astype(BF)
    hg[...] = (gate * hidden).astype(BF)
    dg[...] = d_gate
    du[...] = d_up
    outs = (r_own, r_left, r_right, r_fa, r_fb)

    def put(cols, v):
        for out, spans in zip(outs, per_x):
            at = 0
            for start, n in spans:
                out[at : at + n, cols] = v[start : start + n].astype(out.dtype)
                at += n

    for j in range(0, width, block):
        cols = slice(j, j + block)
        put(cols, dot(d_gate, wg[:, cols]) + dot(d_up, wu[:, cols]))
    put(slice(width, width + PAD), jnp.broadcast_to(router, (router.shape[0], PAD)))


def pass_on(left, right, via_left, via_right, to_left, to_right):
    m = via_left.shape[0]
    to_left[:m] = left[:m]
    to_left[m:] = (left[m:].astype(F32) + via_right[...].astype(F32)).astype(BF)
    to_right[:m] = (right[:m].astype(F32) + via_left[...].astype(F32)).astype(BF)
    to_right[m:] = right[m:]


def add_up(mine, a, b, *outs):
    total = mine[...] + a[...].astype(F32) + b[...].astype(F32)
    slots = outs[0].shape[0]
    for d, out in enumerate(outs):
        out[...] = total[d * slots : (d + 1) * slots].astype(BF)


def combine(width, block, targets, slot_e, ids_e, slot_l, ids_l, e0, e1, e2, e3, l0, l1, l2, l3, keep, send):
    slots = l0.shape[0]
    n = keep.shape[0] // 4
    first = targets[NY] == 0
    narrow = [one_hot(slot[...], slots)[:, : NY * slots] for slot in (slot_e, slot_l)]
    homes = ((e0, e1, e2, e3), (l0, l1, l2, l3))

    def give(cols, e, l):
        e0, em1, ep1, em2 = (e[i * n : (i + 1) * n] for i in range(4))
        lp2, lm3, lp3, l4 = (l[i * n : (i + 1) * n] for i in range(4))
        plus = jnp.concatenate([ep1, lp2, lp3, e0[: n // 2], l4[: n // 2]], axis=0)
        minus = jnp.concatenate([em1, em2, lm3, e0[n // 2 :], l4[n // 2 :]], axis=0)
        keep[:, cols] = jnp.where(first, plus, minus)
        send[:, cols] = jnp.where(first, minus, plus).astype(BF)

    for j in range(0, width, block):
        cols = slice(j, j + block)
        give(cols, *(dot(p, stacked(home, cols)) for p, home in zip(narrow, homes)))
    tails = []
    for p, home, ids in zip(narrow, homes, (ids_e, ids_l)):
        tail = stacked(home, slice(width, width + PAD))
        at = lanes(p.shape)
        routed = jnp.zeros(ids.shape, F32)
        for d in range(NY):
            val = dot(jnp.where(at // slots == d, p, jnp.zeros_like(p)), tail)
            routed = routed + jnp.where(ids[...] == targets[d].astype(F32), val, 0.0)
        tails.append(routed)
    give(slice(width, width + PAD), *tails)


def outer(width, block, many, *refs):
    parts = refs[:many]
    *small, o_gate, o_up, o_down, ready = refs[many:]
    third = len(small) // 3
    share = o_gate.shape[0]
    ready[...] = jnp.zeros(ready.shape, F32)
    every = slice(None)

    def flip(group):
        return stacked(group, every).astype(F32).T.astype(BF)

    turned = jnp.concatenate([flip(small[:third]), flip(small[third : 2 * third])], axis=0)
    turned_h = flip(small[2 * third :])
    for j in range(0, width, block):
        both = dot(turned, stacked(parts, slice(j, j + block))).astype(BF)
        o_gate[:, j : j + block] = both[:share]
        o_up[:, j : j + block] = both[share:]
        y = stacked(parts, slice(width + j, width + j + block))
        o_down[:, j : j + block] = dot(turned_h, y).astype(BF)


def body(tokens, out_grad, expert_ids, gate_values, gate_weight, up_weight, down_weight):
    rows, width = tokens.shape
    top = expert_ids.shape[1]
    share = gate_weight.shape[1]
    full, back_w = 2 * width + PAD, width + PAD
    me = lax.axis_index("expert").astype(jnp.int32)
    my_y, my_zc = me // (NZ * NC), me % (NZ * NC)
    core = me % NC
    targets = jnp.stack([((my_y + d) % NY) * (NZ * NC) + my_zc for d in Y_ORDER] + [core])
    me = me[None]
    wg, wu, wd = gate_weight[0], up_weight[0], down_weight[0]

    extra = jnp.concatenate(
        [expert_ids.astype(BF), gate_values, jnp.zeros((rows, PAD - 2 * top), BF)], axis=1
    )
    pay = jnp.concatenate([tokens, out_grad, extra], axis=1)

    def both(v):
        return move_x(v, 1), move_x(v, -1)

    def onward(near):
        n = near[0].shape[0] // 2
        return move_x(near[0][:n], 1), move_x(near[1][n:], -1)

    across = move(pay, dc=1)
    pair = jnp.concatenate(
        [jnp.where(core == 0, pay, across), jnp.where(core == 0, across, pay)], axis=0
    )
    one, two = move_split(pair, dz=1), move_split(pair, dz=2)
    three = move_split(two, dz=1)
    four = move_split(lax.dynamic_slice_in_dim(two, core * width, width + PAD, 1), dz=2)
    one_o, two_o, three_o, four_o = (move(v, dc=1) for v in (one, two, three, four))
    n = NC * rows
    held = 4 * n
    count = held
    slots = count // rows * CAP

    def early_k(targets, pair, one, one_o, two, two_o, out):
        out[:n] = pair[...]

        def fill(minus, plus, last):
            out[n : 2 * n] = minus[...]
            out[2 * n : 3 * n] = plus[...]
            out[3 * n :] = last[...]

        pl.when(targets[NY] == 0)(lambda: fill(one, one_o, two))
        pl.when(targets[NY] == 1)(lambda: fill(one_o, one, two_o))

    def late_k(targets, two, two_o, three, three_o, four, four_o, out):
        def fill(plus2, minus3, plus3, low, high):
            out[:n] = plus2[...]
            out[n : 2 * n] = minus3[...]
            out[2 * n : 3 * n] = plus3[...]
            out[3 * n :, : width + PAD] = low[...]
            out[3 * n :, width:] = high[...]

        pl.when(targets[NY] == 0)(lambda: fill(two_o, three, three_o, four, four_o))
        pl.when(targets[NY] == 1)(lambda: fill(two, three_o, three, four_o, four))

    moved = 4 * held * full
    (early,) = call(
        early_k, [((held, full), BF)], (targets, pair, one, one_o, two, two_o), 0, moved
    )
    near = move_split(early, dx=1)
    (late,) = call(
        late_k,
        [((held, full), BF)],
        (targets, two, two_o, three, three_o, four, four_o),
        0,
        moved,
    )

    def choosing(groups, into, outs, pieces, first=()):
        def kernel(*refs):
            choose(rows, top, width, tile(full, 1664), groups, slots, into, *refs)

        return call(
            kernel,
            [((n, full), BF) for n in outs] + [((count, PAD), F32)] * 2,
            (targets, *pieces),
            2 * count * PAD * full * len(groups),
            4 * count * full * len(groups),
            first,
        )

    l0, l1, l2, l3, slot_l, ids_l = choosing(
        (1,), [[(d, 0) for d in range(NY)]], [slots] * NY, (late,)
    )
    l1, l2, l3 = move(l1, dy=1), move(l2, dy=-1), move(l3, dy=2)

    def cut(targets, near, half, whole):
        m = half.shape[0]
        whole[...] = near[...]

        def fill(at):
            half[...] = near[at : at + m]

        pl.when(targets[NY] == 0)(lambda: fill(0))
        pl.when(targets[NY] == 1)(lambda: fill(m))

    half, near = call(
        cut,
        [((held // 2, full), BF), ((held, full), BF)],
        (targets, near),
        0,
        moved,
        (slot_l,),
    )
    far = move_split(half, dx=1)

    def hold(far, out):
        out[...] = far[...]

    (far,) = call(hold, [(far.shape, BF)], (far,), 0, moved, (l1, l2, l3))
    near_o, far_o = move(near, dc=1), move(far, dc=1)

    def join(*refs):
        *ins, out = refs
        for i, piece in enumerate(ins):
            out[i * slots : (i + 1) * slots] = piece[...]

    (late,) = call(
        join,
        [((NY * slots, full), BF)],
        (l0, l1, l2, l3),
        0,
        16 * slots * full,
        (far_o,),
    )
    late_near = both(late)
    all_x, part_x = 4 * slots, 2 * slots
    into = [
        [(0, x * slots), (1, x * slots), (2, x * slots), (1 + x // 2, all_x + x % 2 * slots)]
        for x in range(4)
    ]
    e0, e1, e2, slot_e, ids_e = choosing(
        (1, 1, 1, 2),
        into,
        [all_x, all_x + part_x, all_x + part_x],
        (early, near, near_o, far, far_o),
    )
    e1, e2 = move(e1, dy=1), move(e2, dy=-1)
    early_parts = [e0, e1, e2, move(e1[all_x:], dy=1), move(e2[all_x:], dy=-1)]
    early_sizes = [all_x] * 3 + [part_x] * 2
    late_far = onward(late_near)

    def back_and_forth(parts, sizes, per_x, first=()):
        def kernel(*refs):
            expert(top, tile(width, 1024), per_x, sizes, *refs)

        n = sum(sizes)
        r_own, r_left, r_right, r_fa, r_fb, hg, dg, du = call(
            kernel,
            [((n // 4, back_w), F32)]
            + [((n // 4, back_w), BF)] * 2
            + [((n // 8, back_w), BF)] * 2
            + [((n, share), BF)] * 3,
            (me, *parts, wg, wu, wd),
            2 * n * width * share * 5,
            2 * (n * full + n * back_w + 3 * share * width),
            first,
        )
        return (dg, du, hg), r_own, (r_left, r_right, r_fa, r_fb)

    def spans(many, n):
        near = [[(i * 4 * n + x * n, n) for i in range(many)] for x in range(4)]
        if many == 1:
            return near[:3] + [[(3 * n, n // 2)], [(3 * n + n // 2, n // 2)]]
        return near[:3] + [near[3][: many // 2], near[3][many // 2 :]]

    def returning(sums, forth):
        left, right, fa, fb = sums
        to_left, to_right = call(
            pass_on,
            [(left.shape, BF)] * 2,
            (left, right, forth(fa, 1), forth(fb, -1)),
            0,
            12 * left.size,
        )
        return forth(to_left, -1), forth(to_right, 1)

    def split_x(v, d):
        return move_split(v, dx=d)

    late_parts = [late, *late_near, *late_far]
    late_sizes = [p.shape[0] for p in late_parts]
    small_l, own_l, sums = back_and_forth(late_parts, late_sizes, spans(1, NY * slots))
    got_l = returning(sums, move_x)
    small_e, own_e, sums = back_and_forth(early_parts, early_sizes, spans(NY, slots), (own_l,))
    got_e = returning(sums, split_x)

    sizes = late_sizes + early_sizes
    small = [a for group in zip(small_l, small_e) for a in group]

    def outer_k(*refs):
        parts = [p.at[:n] for p, n in zip(refs, sizes)]
        outer(width, tile(width, 512), len(sizes), *parts, *refs[len(sizes) :])

    grad_gate, grad_up, grad_down, ready = call(
        outer_k,
        [((share, width), BF)] * 3 + [((8, PAD), F32)],
        (*late_parts, *early_parts, *small),
        2 * 3 * 8 * count * share * width,
        2 * (8 * count * full + 3 * share * width),
        got_l,
    )

    def home(own, got, first):
        h0, h1, h2, h3 = call(
            add_up,
            [((slots, back_w), BF)] * NY,
            (own, *got),
            0,
            20 * count * back_w,
            first,
        )
        return h0, move(h1, dy=-1), move(h2, dy=1), move(h3, dy=2)

    home_l = home(own_l, got_l, ())
    home_e = home(own_e, got_e, (ready,))

    def combine_k(*refs):
        combine(width, tile(width, 1024), *refs)

    keep, send = call(
        combine_k,
        [((count, back_w), F32), ((count, back_w), BF)],
        (targets, slot_e, ids_e, slot_l, ids_l, *home_e, *home_l),
        4 * count * count * back_w,
        10 * count * back_w,
    )
    cored = keep + move(send, dc=1).astype(F32)
    sent = cored.astype(BF)
    apart = sum(move_split(sent[i * n : (i + 1) * n], dz=i + 1).astype(F32) for i in range(3))
    opposite = move_split(sent[3 * n + rows :], dz=NZ // 2)
    ours = jnp.where(core == 0, apart[:rows], apart[rows:])
    theirs = jnp.where(core == 0, apart[rows:], apart[:rows])

    def finish(mine, opposite, ours, other, token_out, router_out):
        def total(cols):
            far = opposite[:, cols].astype(F32) + other[:, cols].astype(F32)
            return mine[:, cols] + ours[:, cols] + far

        token_out[...] = total(slice(0, width)).astype(BF)
        router_out[...] = total(slice(width, width + PAD))[:, :top]

    token_grad, router_grad = call(
        finish,
        [((rows, width), BF), ((rows, top), F32)],
        (cored[3 * n : 3 * n + rows], opposite, ours, move(theirs.astype(BF), dc=1)),
        0,
        20 * rows * width,
        mib=16,
    )
    return token_grad, router_grad, grad_gate[None], grad_up[None], grad_down[None]


def solution(mesh):
    both = P(("seq", "expert"), None)
    weight = P("expert", "seq", None)
    return jax.shard_map(
        body,
        mesh=mesh,
        in_specs=(both, both, both, both, weight, weight, weight),
        out_specs=(both, both, weight, weight, weight),
        check_vma=False,
    )
```
